32 devices in a mesh: tm: 8 (over z, x), chan: 4 (over y, core).
Axes of the slice: x: 2, y: 2, z: 4, core: 2. Of those that a mesh axis runs over, the one named last changes fastest.
Arguments:
- traces: float32 [4096, 16384], P('tm', 'chan'), may hold values from -6 to 6
- band_edges: int32 [2, 4096], replicated, may hold values from 0 to 8191, as said below
- taps: float32 [255], replicated, may hold values from -0.375 to 0.375
- gain_table: float32 [64], replicated, may hold values from 0.3 to 3
- gain_index: int32 [16384], P('chan'), may hold values from 0 to 63
Outputs:
- filtered: float32 [4096, 16384], P('tm', 'chan')
The draws below stay inside these ranges and needn't reach their ends.
Inputs may be any that keep to these rules, and one draw needn't show every extreme that they name: band_edges[0, f] <= band_edges[1, f] for every f.
All inputs are finite; a program needn't handle non-finite values.
Results may differ from the reference program's by a relative error of at most 0.0001.
Values sent between devices are 32-bit elements; how exact they have to be, the bound alone decides.
A program may use at most 128 MiB of HBM per device.

```python
import math
import jax
import jax.numpy as jnp
from jax import lax

SAMPLES = 4096
CHANNELS = 16384
TAPS = 255
GROUPS = 64


def draw_band_edges(key, part):
    first, second = jax.random.split(key)
    freq = jnp.arange(SAMPLES, dtype=jnp.int32)
    magnitude = jnp.minimum(freq, SAMPLES - freq)
    jitter = jax.random.randint(first, (SAMPLES,), 0, CHANNELS // 128)
    slope = max(1, CHANNELS // SAMPLES)
    high = jnp.minimum(CHANNELS // 2 - 1, CHANNELS // 256 + slope * magnitude + jitter)
    low = jax.random.randint(second, (SAMPLES,), 0, CHANNELS // 256 + 1)
    return jnp.stack([low, high]).astype(jnp.int32)


def touch_ends(array, key, smallest, top_value):
    place = [jax.random.randint(jax.random.fold_in(key, axis), (), 0, length) for axis, length in enumerate(array.shape)]
    longest = array.shape.index(max(array.shape))
    beside = place[:longest] + [(place[longest] + 1) % array.shape[longest]] + place[longest + 1:]
    return array.at[tuple(place)].set(smallest).at[tuple(beside)].set(top_value)


def steps_of(rng, dims, cuts, smallest, high):
    level = 1.0
    for axis_at, shards_of in cuts:
        steps = jax.random.uniform(jax.random.fold_in(jax.random.fold_in(rng, 6), axis_at), (shards_of,), jnp.float32, smallest / len(cuts), high / len(cuts))
        level = level * jnp.repeat(jnp.exp(steps), dims[axis_at] // shards_of).reshape((-1,) + (1,) * (len(dims) - 1 - axis_at))
    return level


def centred(stream_key, dims, spread, bound, pieces=(), kind=jnp.bfloat16):
    values = jax.random.normal(stream_key, dims, jnp.float32) * spread
    if len(pieces) > 0:
        values = steps_of(stream_key, dims, pieces, -0.22, 0.18) * values
    return jnp.clip(values, min=-bound, max=bound).astype(kind)


def setup_inputs(seed: int = 0) -> dict:
    keys = jax.random.split(jax.random.key(seed), 6)
    return {
        "traces": centred(keys[0], (SAMPLES, CHANNELS), 1.0, 6.0, ((0, 8), (1, 4)), jnp.float32),
        "band_edges": draw_band_edges(jax.random.fold_in(keys[5], 71), 0),
        "taps": centred(keys[2], (TAPS,), TAPS ** -0.5, 0.375, (), jnp.float32),
        "gain_table": jnp.clip(jnp.exp(jax.random.uniform(keys[3], (GROUPS,), jnp.float32, math.log(0.3), math.log(3.0))), 0.3, 3.0),
        "gain_index": touch_ends(jax.random.randint(keys[4], (CHANNELS,), 0, GROUPS), jax.random.fold_in(keys[4], 1), 0, GROUPS - 1).astype(jnp.int32),
    }


def toeplitz_tiles(taps):
    count = taps.shape[0]
    centre = (count - 1) // 2
    before = 256 - centre
    after = 512 - before - count
    widened = jnp.concatenate([jnp.zeros((before,), jnp.float32), taps.astype(jnp.float32), jnp.zeros((after,), jnp.float32)])
    tiles = []
    for shift in range(3):
        start = 128 * shift + 128
        reversed_part = widened[start - 127:start + 128][::-1]
        rolled = jnp.concatenate([reversed_part[127:], jnp.zeros((1,), jnp.float32), reversed_part[:127]])
        tiled = jnp.tile(rolled, 128)[: 128 * 255].reshape(128, 255)
        tiles.append(tiled[:, :128])
    return jnp.stack(tiles)


def reference(traces, band_edges, taps, gain_table, gain_index):
    spectrum = jnp.fft.rfft(traces, axis=1)[:, : CHANNELS // 2]
    spectrum = jnp.fft.fft(spectrum, axis=0)
    wave = jnp.arange(CHANNELS // 2, dtype=jnp.int32)[None, :]
    kept = (wave >= band_edges[0][:, None]) & (wave <= band_edges[1][:, None])
    spectrum = jnp.where(kept, spectrum, jnp.zeros_like(spectrum))
    spectrum = jnp.fft.ifft(spectrum, axis=0)
    spectrum = jnp.concatenate([spectrum, jnp.zeros((SAMPLES, 1), spectrum.dtype)], axis=1)
    fanned = jnp.fft.irfft(spectrum, n=CHANNELS, axis=1).astype(jnp.float32)
    padded = jnp.concatenate([jnp.zeros((128, CHANNELS), jnp.float32), fanned, jnp.zeros((128, CHANNELS), jnp.float32)], axis=0)
    tiles = SAMPLES // 128
    blocks = padded.reshape(tiles + 2, 128, CHANNELS)
    kernels = toeplitz_tiles(taps)
    total = jnp.zeros((tiles, 128, CHANNELS), jnp.float32)
    for shift in range(3):
        total = total + jnp.einsum("ab,jac->jbc", kernels[shift], blocks[shift:shift + tiles], precision=lax.Precision.HIGHEST)
    gains = jnp.take(gain_table, gain_index)
    return total.reshape(SAMPLES, CHANNELS) * gains[None, :]
```

```python
import functools
import math

import jax
import jax.numpy as jnp
import ml_dtypes
import numpy as np
from jax import lax
from jax.experimental import pallas as pl
from jax.experimental.pallas import tpu as pltpu
from jax.sharding import PartitionSpec as P

WIDE = 256
LANES = 128
AXES = ("tm", "chan")
F32 = jnp.float32


def halves(table):
    table = np.asarray(table, np.float32)
    high = table.astype(ml_dtypes.bfloat16)
    low = (table - high.astype(np.float32)).astype(ml_dtypes.bfloat16)
    return np.stack([high, low])


def turn(product, period):
    theta = (product % period) * (2.0 * math.pi / period)
    return np.cos(theta), np.sin(theta)


def channel_tables(channels):
    radix = channels // WIDE
    a = np.arange(WIDE)
    cos, sin = turn(a[:, None] * a[None, :], WIDE)
    sign = np.where(a < WIDE // 2, 1.0, -1.0)
    table = np.block([[cos, -sin * sign], [sin, cos * sign]])
    low = np.arange(WIDE // 2)
    cos_0, sin_0 = turn(a[:, None] * low[None, :], WIDE)
    cos_m, sin_m = turn(a[:, None] * (radix // 2 + radix * low)[None, :], channels)
    none = np.zeros_like(cos_0)
    first = np.block([[cos_0, none, -sin_0, none], [none, cos_m, none, -sin_m]])
    cos_t, sin_t = turn(np.arange(radix // 2)[:, None] * a[None, :], channels)
    return table, first, cos_t.astype(np.float32), sin_t.astype(np.float32)


def wave_order(channels):
    radix = channels // WIDE
    h = np.arange(WIDE)
    low = np.arange(WIDE // 2)
    rows = [np.concatenate([radix * low, radix // 2 + radix * low])]
    for g in range(1, radix // 2):
        wave = g + radix * h
        rows.append(np.where(h < WIDE // 2, wave, channels - wave))
    return np.concatenate(rows).astype(np.int32)


def real_forward(x):
    n = len(x)
    if n == 2:
        return [(x[0] + x[1], None), (x[0] - x[1], None)]
    even, odd = real_forward(x[0::2]), real_forward(x[1::2])
    out = [None] * (n // 2 + 1)
    out[0] = (even[0][0] + odd[0][0], None)
    out[n // 2] = (even[0][0] - odd[0][0], None)
    out[n // 4] = (even[n // 4][0], -odd[n // 4][0])
    for k in range(1, n // 4):
        c, s = math.cos(2 * math.pi * k / n), math.sin(2 * math.pi * k / n)
        er, ei = even[k]
        o_r, o_i = odd[k]
        wr, wi = o_r * c + o_i * s, o_i * c - o_r * s
        out[k] = (er + wr, ei + wi)
        out[n // 2 - k] = (er - wr, wi - ei)
    return out


def real_inverse(v):
    n = 2 * (len(v) - 1)
    if n == 2:
        return [v[0][0] + v[1][0], v[0][0] - v[1][0]]
    q = n // 4
    even, odd = [None] * (q + 1), [None] * (q + 1)
    even[0] = (v[0][0] + v[n // 2][0], None)
    odd[0] = (v[0][0] - v[n // 2][0], None)
    even[q] = (v[q][0], None)
    odd[q] = (-v[q][1], None)
    for g in range(1, q):
        c, s = math.cos(2 * math.pi * g / n), math.sin(2 * math.pi * g / n)
        ar, ai = v[g]
        br, bi = v[n // 2 - g]
        even[g] = (ar + br, ai - bi)
        dr, di = ar - br, ai + bi
        odd[g] = (dr * c - di * s, di * c + dr * s)
    out = [None] * n
    out[0::2], out[1::2] = real_inverse(even), real_inverse(odd)
    return out


def complex_short(x, direction):
    n = len(x)
    if n == 1:
        return x
    even, odd = complex_short(x[0::2], direction), complex_short(x[1::2], direction)
    out = [None] * n
    for k in range(n // 2):
        o_r, o_i = odd[k]
        if k == 0:
            wr, wi = o_r, o_i
        elif 4 * k == n:
            wr, wi = -direction * o_i, direction * o_r
        else:
            c = math.cos(2 * math.pi * k / n)
            s = direction * math.sin(2 * math.pi * k / n)
            wr, wi = o_r * c - o_i * s, o_i * c + o_r * s
        er, ei = even[k]
        out[k] = (er + wr, ei + wi)
        out[k + n // 2] = (er - wr, ei - wi)
    return out


def split(x):
    high = x.astype(jnp.bfloat16)
    return high, (x - high.astype(F32)).astype(jnp.bfloat16)


def dot(a, b):
    return jnp.dot(a, b, preferred_element_type=F32)


def dot_right(x, table):
    high, low = split(x)
    return dot(high, table[0]) + (dot(low, table[0]) + dot(high, table[1]))


def dot_left(table, x):
    high, low = split(x)
    return dot(table[0], high) + (dot(table[0], low) + dot(table[1], high))


def forward_kernel(x_ref, table_ref, first_ref, cos_ref, sin_ref, out_ref, held):
    owners, rows, width = x_ref.shape
    slots = held.shape[0]
    per = width // WIDE

    @pl.loop(0, rows // 8)
    def _(tile):
        at = pl.ds(pl.multiple_of(tile * 8, 8), 8)
        for lane in range(0, WIDE, LANES):
            x = [
                x_ref[j, at, pl.ds(b * WIDE + lane, LANES)]
                for j in range(owners)
                for b in range(per)
            ]
            g = real_forward(x)
            held[0, at, pl.ds(lane, LANES)] = g[0][0]
            held[0, at, pl.ds(WIDE + lane, LANES)] = g[slots][0]
            for k in range(1, slots):
                c = cos_ref[pl.ds(k, 1), pl.ds(lane, LANES)]
                s = sin_ref[pl.ds(k, 1), pl.ds(lane, LANES)]
                re, im = g[k]
                held[k, at, pl.ds(lane, LANES)] = re * c + im * s
                held[k, at, pl.ds(WIDE + lane, LANES)] = im * c - re * s

    group = min(8, slots)

    @pl.loop(0, slots // group)
    def _(step):
        at = pl.ds(step * group, group)
        x = held[at].reshape(group * rows, 2 * WIDE)
        y = dot_right(x, table_ref).reshape(group, rows, 2 * WIDE)
        out_ref[at, 0] = y[:, :, :WIDE]
        out_ref[at, 1] = y[:, :, WIDE:]

    y = dot_right(held[0], first_ref)
    out_ref[0, 0] = y[:, :WIDE]
    out_ref[0, 1] = y[:, WIDE:]


def inverse_kernel(x_ref, table_ref, first_ref, cos_ref, sin_ref, gain_ref, out_ref, held):
    owners, rows, width = out_ref.shape
    slots = held.shape[0]
    per = width // WIDE
    group = min(8, slots)

    @pl.loop(0, slots // group)
    def _(step):
        at = pl.ds(step * group, group)
        x = jnp.concatenate([x_ref[at, 0], x_ref[at, 1]], axis=-1)
        y = dot_right(x.reshape(group * rows, 2 * WIDE), table_ref)
        held[at] = y.reshape(group, rows, 2 * WIDE)

    held[0] = dot_right(jnp.concatenate([x_ref[0, 0], x_ref[0, 1]], axis=-1), first_ref)

    @pl.loop(0, rows // 8)
    def _(tile):
        at = pl.ds(pl.multiple_of(tile * 8, 8), 8)
        for lane in range(0, WIDE, LANES):
            v = [(held[0, at, pl.ds(lane, LANES)], None)]
            for k in range(1, slots):
                c = cos_ref[pl.ds(k, 1), pl.ds(lane, LANES)]
                s = sin_ref[pl.ds(k, 1), pl.ds(lane, LANES)]
                re = held[k, at, pl.ds(lane, LANES)]
                im = held[k, at, pl.ds(WIDE + lane, LANES)]
                v.append((re * c - im * s, im * c + re * s))
            v.append((held[0, at, pl.ds(WIDE + lane, LANES)], None))
            y = real_inverse(v)
            for j in range(owners):
                for b in range(per):
                    place = pl.ds(b * WIDE + lane, LANES)
                    gain = gain_ref[pl.ds(j, 1), place]
                    out_ref[j, at, place] = y[j * per + b] * gain


def whole(shape):
    return pl.BlockSpec(shape, lambda i: (0,) * len(shape))


def params():
    return pltpu.CompilerParams(vmem_limit_bytes=56 * 2**20)


def channel_forward(x):
    owners, rows, width = x.shape
    channels = owners * width
    slots = channels // WIDE // 2
    block = min(32, rows)
    table, first, cos, sin = channel_tables(channels)
    tables = [jnp.asarray(halves(table)), jnp.asarray(halves(first)), jnp.asarray(cos), jnp.asarray(sin)]
    return pl.pallas_call(
        forward_kernel,
        grid=(rows // block,),
        in_specs=[pl.BlockSpec((owners, block, width), lambda i: (0, i, 0))]
        + [whole(t.shape) for t in tables],
        out_specs=pl.BlockSpec((slots, 2, block, WIDE), lambda i: (0, 0, i, 0)),
        out_shape=jax.ShapeDtypeStruct((slots, 2, rows, WIDE), F32),
        scratch_shapes=[pltpu.VMEM((slots, block, 2 * WIDE), F32)],
        compiler_params=params(),
        name="channel_forward",
    )(x, *tables)


def channel_inverse(x, gains, owners):
    slots, _, rows, _ = x.shape
    channels = 2 * slots * WIDE
    width = channels // owners
    block = min(32, rows)
    table, first, cos, sin = channel_tables(channels)
    tables = [jnp.asarray(halves(table.T)), jnp.asarray(halves(first.T)), jnp.asarray(cos), jnp.asarray(sin), gains]
    return pl.pallas_call(
        inverse_kernel,
        grid=(rows // block,),
        in_specs=[pl.BlockSpec((slots, 2, block, WIDE), lambda i: (0, 0, i, 0))]
        + [whole(t.shape) for t in tables],
        out_specs=pl.BlockSpec((owners, block, width), lambda i: (0, i, 0)),
        out_shape=jax.ShapeDtypeStruct((owners, rows, width), F32),
        scratch_shapes=[pltpu.VMEM((slots, block, 2 * WIDE), F32)],
        compiler_params=params(),
        name="channel_inverse",
    )(x, *tables)


def time_kernel(x_ref, table_ref, cos_ref, sin_ref, factor_ref, fir_ref, out_ref, held, line):
    devices, _, rows, lanes = x_ref.shape
    radix = held.shape[1]
    per = WIDE // rows

    for part in range(per):
        @pl.loop(0, rows // 8)
        def _(tile):
            at = pl.ds(pl.multiple_of(tile * 8, 8), 8)
            to = pl.ds(pl.multiple_of(part * rows + tile * 8, 8), 8)
            x = [(x_ref[b * per + part, 0, at], x_ref[b * per + part, 1, at]) for b in range(radix)]
            y = complex_short(x, -1.0)
            for g in range(radix):
                re, im = y[g]
                c, s = cos_ref[g, to], sin_ref[g, to]
                held[0, g, to] = re * c + im * s
                held[1, g, to] = im * c - re * s

    @pl.loop(0, radix)
    def _(g):
        y = dot_left(table_ref, jnp.concatenate([held[0, g], held[1, g]], axis=1))
        factor = factor_ref[g]
        re = (y[:WIDE, :lanes] + y[WIDE:, lanes:]) * factor
        im = (y[:WIDE, lanes:] - y[WIDE:, :lanes]) * factor
        y = dot_left(table_ref, jnp.concatenate([re, im], axis=1))
        re = y[:WIDE, :lanes] - y[WIDE:, lanes:]
        im = y[:WIDE, lanes:] + y[WIDE:, :lanes]
        c, s = cos_ref[g], sin_ref[g]
        held[0, g] = re * c - im * s
        held[1, g] = im * c + re * s

    edge = line.shape[1] - LANES
    for part in range(2):
        line[part, :LANES] = jnp.zeros((LANES, lanes), F32)
        line[part, edge:] = jnp.zeros((LANES, lanes), F32)

    @pl.loop(0, WIDE // 8)
    def _(tile):
        at = pl.ds(pl.multiple_of(tile * 8, 8), 8)
        y = complex_short([(held[0, g, at], held[1, g, at]) for g in range(radix)], 1.0)
        for b in range(radix):
            to = pl.ds(pl.multiple_of(LANES + b * WIDE + tile * 8, 8), 8)
            line[0, to] = y[b][0]
            line[1, to] = y[b][1]

    @pl.loop(0, radix)
    def _(b):
        at = pl.ds(pl.multiple_of(b * WIDE, WIDE), 2 * WIDE)
        y = dot_left(fir_ref, jnp.concatenate([line[0, at], line[1, at]], axis=1))
        to = pl.ds(b * per, per)
        out_ref[to, 0] = y[:, :lanes].reshape(per, rows, lanes)
        out_ref[to, 1] = y[:, lanes:].reshape(per, rows, lanes)


def fir_table(taps):
    count = taps.shape[0]
    shift = LANES - (count - 1) // 2
    period = 2 * WIDE + 1
    row = jnp.pad(taps, (shift, period - count - shift))
    table = jnp.tile(row, WIDE)[: WIDE * 2 * WIDE].reshape(WIDE, 2 * WIDE)
    high = lax.reduce_precision(table, 8, 7)
    return jnp.stack([high, table - high]).astype(jnp.bfloat16)


def time_stage(x, factor, taps):
    devices, _, rows, piece = x.shape
    samples = devices * rows
    radix = samples // WIDE
    a = np.arange(WIDE)
    cos, sin = turn(a[:, None] * a[None, :], WIDE)
    table = jnp.asarray(halves(np.concatenate([cos, sin], axis=0)))
    cos_t, sin_t = turn(np.arange(radix)[:, None] * a[None, :], samples)
    turns = [
        jnp.broadcast_to(jnp.asarray(t.astype(np.float32))[:, :, None], (radix, WIDE, LANES))
        for t in (cos_t, sin_t)
    ]
    fir = fir_table(taps)
    block = pl.BlockSpec((devices, 2, rows, LANES), lambda i: (0, 0, 0, i))
    return pl.pallas_call(
        time_kernel,
        grid=(piece // LANES,),
        in_specs=[
            block,
            whole(table.shape),
            whole(turns[0].shape),
            whole(turns[1].shape),
            pl.BlockSpec((radix, WIDE, LANES), lambda i: (0, 0, i)),
            whole(fir.shape),
        ],
        out_specs=block,
        out_shape=jax.ShapeDtypeStruct(x.shape, F32),
        scratch_shapes=[
            pltpu.VMEM((2, radix, WIDE, LANES), F32),
            pltpu.VMEM((2, samples + 2 * LANES, LANES), F32),
        ],
        compiler_params=params(),
        name="time_stage",
    )(x, table, *turns, factor, fir)


def mask_factor(band_edges, channels, piece, width):
    samples = band_edges.shape[1]
    owner = lax.axis_index("tm") * lax.axis_size("chan") + lax.axis_index("chan")
    order = jnp.asarray(wave_order(channels))
    wave = lax.dynamic_slice_in_dim(order, owner * piece, piece)
    wave = jnp.pad(wave, (0, width - piece))[None, None, :]
    edges = band_edges.reshape(2, WIDE, samples // WIDE).transpose(0, 2, 1)[:, :, :, None]
    kept = (wave >= edges[0]) & (wave <= edges[1])
    weight = jnp.where(wave == 0, 1.0, 2.0).astype(F32)
    return jnp.where(kept, weight, 0.0) / float(samples * channels)


def regroup(x, devices):
    slots, _, rows, _ = x.shape
    share = devices // slots
    if share == 1:
        return x
    x = x.reshape(slots, 2, rows, share, WIDE // share).transpose(0, 3, 1, 2, 4)
    return x.reshape(devices, 2, rows, WIDE // share)


def ungroup(x, slots):
    devices, _, rows, piece = x.shape
    share = devices // slots
    if share == 1:
        return x
    x = x.reshape(slots, share, 2, rows, piece).transpose(0, 2, 3, 1, 4)
    return x.reshape(slots, 2, rows, WIDE)


def exchange(x, axes):
    return lax.all_to_all(x, axes, split_axis=0, concat_axis=0, tiled=True)


def per_device(traces, band_edges, taps, gain_table, gain_index):
    owners = lax.axis_size("chan")
    devices = lax.axis_size("tm") * owners
    length, width = traces.shape
    channels = owners * width
    slots = channels // WIDE // 2
    piece = channels // 2 // devices
    padded = max(piece, LANES)
    matches = gain_index[:, None] == jnp.arange(gain_table.shape[0], dtype=jnp.int32)[None, :]
    gains = jnp.sum(jnp.where(matches, gain_table[None, :], 0.0), axis=1)
    gains = lax.all_gather(gains, "chan")
    factor = mask_factor(band_edges, channels, piece, padded)

    gathered = exchange(traces.reshape(owners, length // owners, width), "chan")
    spectra = exchange(regroup(channel_forward(gathered), devices), AXES)
    if padded > piece:
        spectra = jnp.pad(spectra, ((0, 0), (0, 0), (0, 0), (0, padded - piece)))
    spectra = time_stage(spectra, factor, taps)
    if padded > piece:
        spectra = spectra[..., :piece]
    returned = ungroup(exchange(spectra, AXES), slots)
    local = exchange(channel_inverse(returned, gains, owners), "chan")
    return local.reshape(length, width)


def solution(mesh):
    in_specs = (P("tm", "chan"), P(), P(), P(), P("chan"))
    out_specs = P("tm", "chan")
    return jax.shard_map(
        per_device, mesh=mesh, in_specs=in_specs, out_specs=out_specs, check_vma=False
    )
```

```python
import functools
import math

import jax
import jax.numpy as jnp
import ml_dtypes
import numpy as np
from jax import lax
from jax.experimental import pallas as pl
from jax.experimental.pallas import tpu as pltpu
from jax.sharding import PartitionSpec as P

WIDE = 256
LANES = 128
AXES = ("tm", "chan")
F32 = jnp.float32


def halves(table):
    table = np.asarray(table, np.float32)
    high = table.astype(ml_dtypes.bfloat16)
    low = (table - high.astype(np.float32)).astype(ml_dtypes.bfloat16)
    return np.stack([high, low])


def turn(product, period):
    theta = (product % period) * (2.0 * math.pi / period)
    return np.cos(theta), np.sin(theta)


def channel_tables(channels):
    radix = channels // WIDE
    a = np.arange(WIDE)
    cos, sin = turn(a[:, None] * a[None, :], WIDE)
    sign = np.where(a < WIDE // 2, 1.0, -1.0)
    table = np.block([[cos, -sin * sign], [sin, cos * sign]])
    low = np.arange(WIDE // 2)
    cos_0, sin_0 = turn(a[:, None] * low[None, :], WIDE)
    cos_m, sin_m = turn(a[:, None] * (radix // 2 + radix * low)[None, :], channels)
    none = np.zeros_like(cos_0)
    first = np.block([[cos_0, none, -sin_0, none], [none, cos_m, none, -sin_m]])
    cos_t, sin_t = turn(np.arange(radix // 2)[:, None] * a[None, :], channels)
    return table, first, cos_t.astype(np.float32), sin_t.astype(np.float32)


def wave_order(channels):
    radix = channels // WIDE
    h = np.arange(WIDE)
    low = np.arange(WIDE // 2)
    rows = [np.concatenate([radix * low, radix // 2 + radix * low])]
    for g in range(1, radix // 2):
        wave = g + radix * h
        rows.append(np.where(h < WIDE // 2, wave, channels - wave))
    return np.concatenate(rows).astype(np.int32)


def real_forward(x):
    n = len(x)
    if n == 2:
        return [(x[0] + x[1], None), (x[0] - x[1], None)]
    even, odd = real_forward(x[0::2]), real_forward(x[1::2])
    out = [None] * (n // 2 + 1)
    out[0] = (even[0][0] + odd[0][0], None)
    out[n // 2] = (even[0][0] - odd[0][0], None)
    out[n // 4] = (even[n // 4][0], -odd[n // 4][0])
    for k in range(1, n // 4):
        c, s = math.cos(2 * math.pi * k / n), math.sin(2 * math.pi * k / n)
        er, ei = even[k]
        o_r, o_i = odd[k]
        wr, wi = o_r * c + o_i * s, o_i * c - o_r * s
        out[k] = (er + wr, ei + wi)
        out[n // 2 - k] = (er - wr, wi - ei)
    return out


def real_inverse(v):
    n = 2 * (len(v) - 1)
    if n == 2:
        return [v[0][0] + v[1][0], v[0][0] - v[1][0]]
    q = n // 4
    even, odd = [None] * (q + 1), [None] * (q + 1)
    even[0] = (v[0][0] + v[n // 2][0], None)
    odd[0] = (v[0][0] - v[n // 2][0], None)
    even[q] = (v[q][0], None)
    odd[q] = (-v[q][1], None)
    for g in range(1, q):
        c, s = math.cos(2 * math.pi * g / n), math.sin(2 * math.pi * g / n)
        ar, ai = v[g]
        br, bi = v[n // 2 - g]
        even[g] = (ar + br, ai - bi)
        dr, di = ar - br, ai + bi
        odd[g] = (dr * c - di * s, di * c + dr * s)
    out = [None] * n
    out[0::2], out[1::2] = real_inverse(even), real_inverse(odd)
    return out


def complex_short(x, direction):
    n = len(x)
    if n == 1:
        return x
    even, odd = complex_short(x[0::2], direction), complex_short(x[1::2], direction)
    out = [None] * n
    for k in range(n // 2):
        o_r, o_i = odd[k]
        if k == 0:
            wr, wi = o_r, o_i
        elif 4 * k == n:
            wr, wi = -direction * o_i, direction * o_r
        else:
            c = math.cos(2 * math.pi * k / n)
            s = direction * math.sin(2 * math.pi * k / n)
            wr, wi = o_r * c - o_i * s, o_i * c + o_r * s
        er, ei = even[k]
        out[k] = (er + wr, ei + wi)
        out[k + n // 2] = (er - wr, ei - wi)
    return out


def split(x):
    high = x.astype(jnp.bfloat16)
    return high, (x - high.astype(F32)).astype(jnp.bfloat16)


def dot(a, b):
    return jnp.dot(a, b, preferred_element_type=F32)


def dot_right(x, table):
    high, low = split(x)
    return dot(high, table[0]) + (dot(low, table[0]) + dot(high, table[1]))


def dot_left(table, x):
    high, low = split(x)
    return dot(table[0], high) + (dot(table[0], low) + dot(table[1], high))


def forward_kernel(x_ref, table_ref, first_ref, cos_ref, sin_ref, out_ref, held):
    owners, rows, width = x_ref.shape
    slots = held.shape[0]
    per = width // WIDE

    @pl.loop(0, rows // 8)
    def _(tile):
        at = pl.ds(pl.multiple_of(tile * 8, 8), 8)
        for lane in range(0, WIDE, LANES):
            x = [
                x_ref[j, at, pl.ds(b * WIDE + lane, LANES)]
                for j in range(owners)
                for b in range(per)
            ]
            g = real_forward(x)
            held[0, at, pl.ds(lane, LANES)] = g[0][0]
            held[0, at, pl.ds(WIDE + lane, LANES)] = g[slots][0]
            for k in range(1, slots):
                c = cos_ref[pl.ds(k, 1), pl.ds(lane, LANES)]
                s = sin_ref[pl.ds(k, 1), pl.ds(lane, LANES)]
                re, im = g[k]
                held[k, at, pl.ds(lane, LANES)] = re * c + im * s
                held[k, at, pl.ds(WIDE + lane, LANES)] = im * c - re * s

    group = min(8, slots)

    @pl.loop(0, slots // group)
    def _(step):
        at = pl.ds(step * group, group)
        x = held[at].reshape(group * rows, 2 * WIDE)
        y = dot_right(x, table_ref).reshape(group, rows, 2 * WIDE)
        out_ref[at, 0] = y[:, :, :WIDE]
        out_ref[at, 1] = y[:, :, WIDE:]

    y = dot_right(held[0], first_ref)
    out_ref[0, 0] = y[:, :WIDE]
    out_ref[0, 1] = y[:, WIDE:]


def inverse_kernel(x_ref, table_ref, first_ref, cos_ref, sin_ref, gain_ref, out_ref, held):
    owners, rows, width = out_ref.shape
    slots = held.shape[0]
    per = width // WIDE
    group = min(8, slots)

    @pl.loop(0, slots // group)
    def _(step):
        at = pl.ds(step * group, group)
        x = jnp.concatenate([x_ref[at, 0], x_ref[at, 1]], axis=-1)
        y = dot_right(x.reshape(group * rows, 2 * WIDE), table_ref)
        held[at] = y.reshape(group, rows, 2 * WIDE)

    held[0] = dot_right(jnp.concatenate([x_ref[0, 0], x_ref[0, 1]], axis=-1), first_ref)

    @pl.loop(0, rows // 8)
    def _(tile):
        at = pl.ds(pl.multiple_of(tile * 8, 8), 8)
        for lane in range(0, WIDE, LANES):
            v = [(held[0, at, pl.ds(lane, LANES)], None)]
            for k in range(1, slots):
                c = cos_ref[pl.ds(k, 1), pl.ds(lane, LANES)]
                s = sin_ref[pl.ds(k, 1), pl.ds(lane, LANES)]
                re = held[k, at, pl.ds(lane, LANES)]
                im = held[k, at, pl.ds(WIDE + lane, LANES)]
                v.append((re * c - im * s, im * c + re * s))
            v.append((held[0, at, pl.ds(WIDE + lane, LANES)], None))
            y = real_inverse(v)
            for j in range(owners):
                for b in range(per):
                    place = pl.ds(b * WIDE + lane, LANES)
                    gain = gain_ref[pl.ds(j, 1), place]
                    out_ref[j, at, place] = y[j * per + b] * gain


def whole(shape):
    return pl.BlockSpec(shape, lambda i: (0,) * len(shape))


def params():
    return pltpu.CompilerParams(vmem_limit_bytes=56 * 2**20)


def channel_forward(x):
    owners, rows, width = x.shape
    channels = owners * width
    slots = channels // WIDE // 2
    block = min(32, rows)
    table, first, cos, sin = channel_tables(channels)
    tables = [jnp.asarray(halves(table)), jnp.asarray(halves(first)), jnp.asarray(cos), jnp.asarray(sin)]
    return pl.pallas_call(
        forward_kernel,
        grid=(rows // block,),
        in_specs=[pl.BlockSpec((owners, block, width), lambda i: (0, i, 0))]
        + [whole(t.shape) for t in tables],
        out_specs=pl.BlockSpec((slots, 2, block, WIDE), lambda i: (0, 0, i, 0)),
        out_shape=jax.ShapeDtypeStruct((slots, 2, rows, WIDE), F32),
        scratch_shapes=[pltpu.VMEM((slots, block, 2 * WIDE), F32)],
        compiler_params=params(),
        name="channel_forward",
    )(x, *tables)


def channel_inverse(x, gains, owners):
    slots, _, rows, _ = x.shape
    channels = 2 * slots * WIDE
    width = channels // owners
    block = min(32, rows)
    table, first, cos, sin = channel_tables(channels)
    tables = [jnp.asarray(halves(table.T)), jnp.asarray(halves(first.T)), jnp.asarray(cos), jnp.asarray(sin), gains]
    return pl.pallas_call(
        inverse_kernel,
        grid=(rows // block,),
        in_specs=[pl.BlockSpec((slots, 2, block, WIDE), lambda i: (0, 0, i, 0))]
        + [whole(t.shape) for t in tables],
        out_specs=pl.BlockSpec((owners, block, width), lambda i: (0, i, 0)),
        out_shape=jax.ShapeDtypeStruct((owners, rows, width), F32),
        scratch_shapes=[pltpu.VMEM((slots, block, 2 * WIDE), F32)],
        compiler_params=params(),
        name="channel_inverse",
    )(x, *tables)


def others(devices, visit):
    spread = math.gcd(4, devices)

    @pl.loop(1, devices)
    def _(i):
        visit(lax.rem(i, spread) * (devices // spread) + i // spread)


def greet(devices, owners, me):
    barrier = pltpu.get_barrier_semaphore()

    def hail(step):
        to = lax.rem(me + step, devices)
        pl.semaphore_signal(
            barrier, inc=1, device_id=(to // owners, lax.rem(to, owners)),
            device_id_type=pl.DeviceIdType.MESH,
        )

    others(devices, hail)
    pl.semaphore_wait(barrier, devices - 1)


def send_out_kernel(
    x_ref, table_ref, first_ref, cos_ref, sin_ref, out_ref,
    got, held, ready, own_in, own_out, chan_send, chan_recv, full_send, full_recv,
):
    owners, rows, _ = x_ref.shape
    chunks, devices, _, block, _ = ready.shape
    line, place = lax.axis_index("tm"), lax.axis_index("chan")
    me = line * owners + place

    def part(q):
        return pl.ds(pl.multiple_of(q * block, block), block)

    def across(q, step, back=False):
        to = lax.rem(place + step, owners)
        source = lax.rem(place + owners - step, owners) if back else place
        return pltpu.make_async_remote_copy(
            src_ref=x_ref.at[to, part(q)], dst_ref=got.at[source, part(q)],
            send_sem=chan_send.at[q, step], recv_sem=chan_recv.at[q, step],
            device_id=(line, to), device_id_type=pl.DeviceIdType.MESH,
        )

    def everywhere(q, step, back=False):
        to = lax.rem(me + step, devices)
        source = lax.rem(me + devices - step, devices) if back else me
        return pltpu.make_async_remote_copy(
            src_ref=ready.at[q, to], dst_ref=out_ref.at[source, :, part(q)],
            send_sem=full_send.at[q, step], recv_sem=full_recv.at[q, step],
            device_id=(to // owners, lax.rem(to, owners)), device_id_type=pl.DeviceIdType.MESH,
        )

    def take_own(q):
        return pltpu.make_async_copy(x_ref.at[place, part(q)], got.at[place, part(q)], own_in.at[q])

    def give_own(q):
        return pltpu.make_async_copy(ready.at[q, me], out_ref.at[me, :, part(q)], own_out.at[q])

    def begin(q):
        take_own(q).start()
        for step in range(1, owners):
            across(q, step).start()

    greet(devices, owners, me)
    ahead = min(2, chunks)
    for q in range(ahead):
        begin(q)

    @pl.loop(0, chunks)
    def _(q):
        take_own(q).wait()
        for step in range(1, owners):
            across(q, step, True).wait_recv()

        @pl.when(q + ahead < chunks)
        def _():
            begin(q + ahead)

        forward_kernel(
            got.at[:, part(q)], table_ref, first_ref, cos_ref, sin_ref, ready.at[q], held
        )
        give_own(q).start()
        others(devices, lambda step: everywhere(q, step).start())

    @pl.loop(0, chunks)
    def _(q):
        for step in range(1, owners):
            across(q, step).wait_send()
        give_own(q).wait()

        def finish(step):
            everywhere(q, step).wait_send()
            everywhere(q, step, True).wait_recv()

        others(devices, finish)


def send_back_kernel(
    x_ref, table_ref, first_ref, cos_ref, sin_ref, gain_ref, out_ref,
    got, held, ready, own_in, own_out, chan_send, chan_recv, full_send, full_recv,
):
    owners, rows, _ = out_ref.shape
    devices = x_ref.shape[0]
    chunks = own_in.shape[0]
    block = rows // chunks
    line, place = lax.axis_index("tm"), lax.axis_index("chan")
    me = line * owners + place

    def part(q):
        return pl.ds(pl.multiple_of(q * block, block), block)

    def across(q, step, back=False):
        to = lax.rem(place + step, owners)
        source = lax.rem(place + owners - step, owners) if back else place
        return pltpu.make_async_remote_copy(
            src_ref=ready.at[to, part(q)], dst_ref=out_ref.at[source, part(q)],
            send_sem=chan_send.at[q, step], recv_sem=chan_recv.at[q, step],
            device_id=(line, to), device_id_type=pl.DeviceIdType.MESH,
        )

    def everywhere(q, step, back=False):
        to = lax.rem(me + step, devices)
        source = lax.rem(me + devices - step, devices) if back else me
        return pltpu.make_async_remote_copy(
            src_ref=x_ref.at[to, :, part(q)], dst_ref=got.at[source, :, part(q)],
            send_sem=full_send.at[q, step], recv_sem=full_recv.at[q, step],
            device_id=(to // owners, lax.rem(to, owners)), device_id_type=pl.DeviceIdType.MESH,
        )

    def take_own(q):
        return pltpu.make_async_copy(x_ref.at[me, :, part(q)], got.at[me, :, part(q)], own_in.at[q])

    def give_own(q):
        return pltpu.make_async_copy(ready.at[place, part(q)], out_ref.at[place, part(q)], own_out.at[q])

    def begin(q):
        take_own(q).start()
        others(devices, lambda step: everywhere(q, step).start())

    greet(devices, owners, me)
    ahead = min(2, chunks)
    for q in range(ahead):
        begin(q)

    @pl.loop(0, chunks)
    def _(q):
        take_own(q).wait()
        others(devices, lambda step: everywhere(q, step, True).wait_recv())

        @pl.when(q + ahead < chunks)
        def _():
            begin(q + ahead)

        inverse_kernel(
            got.at[:, :, part(q)], table_ref, first_ref, cos_ref, sin_ref, gain_ref,
            ready.at[:, part(q)], held,
        )
        give_own(q).start()
        for step in range(1, owners):
            across(q, step).start()

    @pl.loop(0, chunks)
    def _(q):
        others(devices, lambda step: everywhere(q, step).wait_send())
        give_own(q).wait()
        for step in range(1, owners):
            across(q, step).wait_send()
            across(q, step, True).wait_recv()


CHUNK = 32


def exchange_semaphores(chunks, owners, devices):
    dma = pltpu.SemaphoreType.DMA
    return [
        dma((chunks,)), dma((chunks,)), dma((chunks, owners)), dma((chunks, owners)),
        dma((chunks, devices)), dma((chunks, devices)),
    ]


def exchange_call(kernel, ident, operands, out_shape, buffers, sizes):
    anywhere = pl.BlockSpec(memory_space=pl.ANY)
    inside = pl.BlockSpec(memory_space=pltpu.VMEM)
    return pl.pallas_call(
        kernel,
        in_specs=[anywhere] + [inside] * (len(operands) - 1),
        out_specs=anywhere,
        out_shape=jax.ShapeDtypeStruct(out_shape, F32),
        scratch_shapes=[pltpu.VMEM(b, F32) for b in buffers] + exchange_semaphores(*sizes),
        compiler_params=pltpu.CompilerParams(
            vmem_limit_bytes=56 * 2**20, collective_id=ident, has_side_effects=True
        ),
        name=kernel.__name__,
    )(*operands)


def send_out(x, devices):
    owners, rows, width = x.shape
    channels = owners * width
    slots = channels // WIDE // 2
    chunks = rows // min(CHUNK, rows)
    block = rows // chunks
    table, first, cos, sin = channel_tables(channels)
    operands = [x] + [jnp.asarray(t) for t in (halves(table), halves(first), cos, sin)]
    buffers = [(owners, rows, width), (slots, block, 2 * WIDE), (chunks, slots, 2, block, WIDE)]
    return exchange_call(
        send_out_kernel, 0, operands, (devices, 2, rows, WIDE), buffers, (chunks, owners, devices)
    )


def send_back(x, gains, owners):
    slots, _, rows, _ = x.shape
    channels = 2 * slots * WIDE
    width = channels // owners
    chunks = rows // min(CHUNK, rows)
    block = rows // chunks
    table, first, cos, sin = channel_tables(channels)
    operands = [x] + [jnp.asarray(t) for t in (halves(table.T), halves(first.T), cos, sin)] + [gains]
    buffers = [x.shape, (slots, block, 2 * WIDE), (owners, rows, width)]
    return exchange_call(
        send_back_kernel, 1, operands, (owners, rows, width), buffers, (chunks, owners, slots)
    )


def time_kernel(x_ref, table_ref, cos_ref, sin_ref, factor_ref, fir_ref, out_ref, held, line):
    devices, _, rows, lanes = x_ref.shape
    radix = held.shape[1]
    per = WIDE // rows

    for part in range(per):
        @pl.loop(0, rows // 8)
        def _(tile):
            at = pl.ds(pl.multiple_of(tile * 8, 8), 8)
            to = pl.ds(pl.multiple_of(part * rows + tile * 8, 8), 8)
            x = [(x_ref[b * per + part, 0, at], x_ref[b * per + part, 1, at]) for b in range(radix)]
            y = complex_short(x, -1.0)
            for g in range(radix):
                re, im = y[g]
                c, s = cos_ref[g, to], sin_ref[g, to]
                held[0, g, to] = re * c + im * s
                held[1, g, to] = im * c - re * s

    @pl.loop(0, radix)
    def _(g):
        y = dot_left(table_ref, jnp.concatenate([held[0, g], held[1, g]], axis=1))
        factor = factor_ref[g]
        re = (y[:WIDE, :lanes] + y[WIDE:, lanes:]) * factor
        im = (y[:WIDE, lanes:] - y[WIDE:, :lanes]) * factor
        y = dot_left(table_ref, jnp.concatenate([re, im], axis=1))
        re = y[:WIDE, :lanes] - y[WIDE:, lanes:]
        im = y[:WIDE, lanes:] + y[WIDE:, :lanes]
        c, s = cos_ref[g], sin_ref[g]
        held[0, g] = re * c - im * s
        held[1, g] = im * c + re * s

    edge = line.shape[1] - LANES
    for part in range(2):
        line[part, :LANES] = jnp.zeros((LANES, lanes), F32)
        line[part, edge:] = jnp.zeros((LANES, lanes), F32)

    @pl.loop(0, WIDE // 8)
    def _(tile):
        at = pl.ds(pl.multiple_of(tile * 8, 8), 8)
        y = complex_short([(held[0, g, at], held[1, g, at]) for g in range(radix)], 1.0)
        for b in range(radix):
            to = pl.ds(pl.multiple_of(LANES + b * WIDE + tile * 8, 8), 8)
            line[0, to] = y[b][0]
            line[1, to] = y[b][1]

    @pl.loop(0, radix)
    def _(b):
        at = pl.ds(pl.multiple_of(b * WIDE, WIDE), 2 * WIDE)
        y = dot_left(fir_ref, jnp.concatenate([line[0, at], line[1, at]], axis=1))
        to = pl.ds(b * per, per)
        out_ref[to, 0] = y[:, :lanes].reshape(per, rows, lanes)
        out_ref[to, 1] = y[:, lanes:].reshape(per, rows, lanes)


def fir_table(taps):
    count = taps.shape[0]
    shift = LANES - (count - 1) // 2
    period = 2 * WIDE + 1
    row = jnp.pad(taps, (shift, period - count - shift))
    table = jnp.tile(row, WIDE)[: WIDE * 2 * WIDE].reshape(WIDE, 2 * WIDE)
    high = lax.reduce_precision(table, 8, 7)
    return jnp.stack([high, table - high]).astype(jnp.bfloat16)


def time_stage(x, factor, taps):
    devices, _, rows, piece = x.shape
    samples = devices * rows
    radix = samples // WIDE
    a = np.arange(WIDE)
    cos, sin = turn(a[:, None] * a[None, :], WIDE)
    table = jnp.asarray(halves(np.concatenate([cos, sin], axis=0)))
    cos_t, sin_t = turn(np.arange(radix)[:, None] * a[None, :], samples)
    turns = [
        jnp.broadcast_to(jnp.asarray(t.astype(np.float32))[:, :, None], (radix, WIDE, LANES))
        for t in (cos_t, sin_t)
    ]
    fir = fir_table(taps)
    block = pl.BlockSpec((devices, 2, rows, LANES), lambda i: (0, 0, 0, i))
    return pl.pallas_call(
        time_kernel,
        grid=(piece // LANES,),
        in_specs=[
            block,
            whole(table.shape),
            whole(turns[0].shape),
            whole(turns[1].shape),
            pl.BlockSpec((radix, WIDE, LANES), lambda i: (0, 0, i)),
            whole(fir.shape),
        ],
        out_specs=block,
        out_shape=jax.ShapeDtypeStruct(x.shape, F32),
        scratch_shapes=[
            pltpu.VMEM((2, radix, WIDE, LANES), F32),
            pltpu.VMEM((2, samples + 2 * LANES, LANES), F32),
        ],
        compiler_params=params(),
        name="time_stage",
    )(x, table, *turns, factor, fir)


def mask_factor(band_edges, channels, piece, width):
    samples = band_edges.shape[1]
    owner = lax.axis_index("tm") * lax.axis_size("chan") + lax.axis_index("chan")
    order = jnp.asarray(wave_order(channels))
    wave = lax.dynamic_slice_in_dim(order, owner * piece, piece)
    wave = jnp.pad(wave, (0, width - piece))[None, None, :]
    edges = band_edges.reshape(2, WIDE, samples // WIDE).transpose(0, 2, 1)[:, :, :, None]
    kept = (wave >= edges[0]) & (wave <= edges[1])
    weight = jnp.where(wave == 0, 1.0, 2.0).astype(F32)
    return jnp.where(kept, weight, 0.0) / float(samples * channels)


def regroup(x, devices):
    slots, _, rows, _ = x.shape
    share = devices // slots
    if share == 1:
        return x
    x = x.reshape(slots, 2, rows, share, WIDE // share).transpose(0, 3, 1, 2, 4)
    return x.reshape(devices, 2, rows, WIDE // share)


def ungroup(x, slots):
    devices, _, rows, piece = x.shape
    share = devices // slots
    if share == 1:
        return x
    x = x.reshape(slots, share, 2, rows, piece).transpose(0, 2, 3, 1, 4)
    return x.reshape(slots, 2, rows, WIDE)


def exchange(x, axes):
    return lax.all_to_all(x, axes, split_axis=0, concat_axis=0, tiled=True)


def per_device(traces, band_edges, taps, gain_table, gain_index):
    owners = lax.axis_size("chan")
    devices = lax.axis_size("tm") * owners
    length, width = traces.shape
    channels = owners * width
    slots = channels // WIDE // 2
    piece = channels // 2 // devices
    padded = max(piece, LANES)
    matches = gain_index[:, None] == jnp.arange(gain_table.shape[0], dtype=jnp.int32)[None, :]
    gains = jnp.sum(jnp.where(matches, gain_table[None, :], 0.0), axis=1)
    gains = lax.all_gather(gains, "chan")
    factor = mask_factor(band_edges, channels, piece, padded)

    if devices == slots:
        spectra = send_out(traces.reshape(owners, length // owners, width), devices)
        spectra = time_stage(spectra, factor, taps)
        return send_back(spectra, gains, owners).reshape(length, width)

    gathered = exchange(traces.reshape(owners, length // owners, width), "chan")
    spectra = exchange(regroup(channel_forward(gathered), devices), AXES)
    if padded > piece:
        spectra = jnp.pad(spectra, ((0, 0), (0, 0), (0, 0), (0, padded - piece)))
    spectra = time_stage(spectra, factor, taps)
    if padded > piece:
        spectra = spectra[..., :piece]
    returned = ungroup(exchange(spectra, AXES), slots)
    local = exchange(channel_inverse(returned, gains, owners), "chan")
    return local.reshape(length, width)


def solution(mesh):
    in_specs = (P("tm", "chan"), P(), P(), P(), P("chan"))
    out_specs = P("tm", "chan")
    return jax.shard_map(
        per_device, mesh=mesh, in_specs=in_specs, out_specs=out_specs, check_vma=False
    )
```

```python
import functools
import math

import jax
import jax.numpy as jnp
import ml_dtypes
import numpy as np
from jax import lax
from jax.experimental import pallas as pl
from jax.experimental.pallas import tpu as pltpu
from jax.sharding import PartitionSpec as P

WIDE = 256
LANES = 128
AXES = ("tm", "chan")
F32 = jnp.float32


def halves(table):
    table = np.asarray(table, np.float32)
    high = table.astype(ml_dtypes.bfloat16)
    low = (table - high.astype(np.float32)).astype(ml_dtypes.bfloat16)
    return np.stack([high, low])


def turn(product, period):
    theta = (product % period) * (2.0 * math.pi / period)
    return np.cos(theta), np.sin(theta)


def channel_tables(channels):
    radix = channels // WIDE
    a = np.arange(WIDE)
    cos, sin = turn(a[:, None] * a[None, :], WIDE)
    sign = np.where(a < WIDE // 2, 1.0, -1.0)
    table = np.block([[cos, -sin * sign], [sin, cos * sign]])
    low = np.arange(WIDE // 2)
    cos_0, sin_0 = turn(a[:, None] * low[None, :], WIDE)
    cos_m, sin_m = turn(a[:, None] * (radix // 2 + radix * low)[None, :], channels)
    none = np.zeros_like(cos_0)
    first = np.block([[cos_0, none, -sin_0, none], [none, cos_m, none, -sin_m]])
    cos_t, sin_t = turn(np.arange(radix // 2)[:, None] * a[None, :], channels)
    return table, first, cos_t.astype(np.float32), sin_t.astype(np.float32)


def wave_order(channels):
    radix = channels // WIDE
    h = np.arange(WIDE)
    low = np.arange(WIDE // 2)
    rows = [np.concatenate([radix * low, radix // 2 + radix * low])]
    for g in range(1, radix // 2):
        wave = g + radix * h
        rows.append(np.where(h < WIDE // 2, wave, channels - wave))
    return np.concatenate(rows).astype(np.int32)


def real_forward(x):
    n = len(x)
    if n == 2:
        return [(x[0] + x[1], None), (x[0] - x[1], None)]
    even, odd = real_forward(x[0::2]), real_forward(x[1::2])
    out = [None] * (n // 2 + 1)
    out[0] = (even[0][0] + odd[0][0], None)
    out[n // 2] = (even[0][0] - odd[0][0], None)
    out[n // 4] = (even[n // 4][0], -odd[n // 4][0])
    for k in range(1, n // 4):
        c, s = math.cos(2 * math.pi * k / n), math.sin(2 * math.pi * k / n)
        er, ei = even[k]
        o_r, o_i = odd[k]
        wr, wi = o_r * c + o_i * s, o_i * c - o_r * s
        out[k] = (er + wr, ei + wi)
        out[n // 2 - k] = (er - wr, wi - ei)
    return out


def real_inverse(v):
    n = 2 * (len(v) - 1)
    if n == 2:
        return [v[0][0] + v[1][0], v[0][0] - v[1][0]]
    q = n // 4
    even, odd = [None] * (q + 1), [None] * (q + 1)
    even[0] = (v[0][0] + v[n // 2][0], None)
    odd[0] = (v[0][0] - v[n // 2][0], None)
    even[q] = (v[q][0], None)
    odd[q] = (-v[q][1], None)
    for g in range(1, q):
        c, s = math.cos(2 * math.pi * g / n), math.sin(2 * math.pi * g / n)
        ar, ai = v[g]
        br, bi = v[n // 2 - g]
        even[g] = (ar + br, ai - bi)
        dr, di = ar - br, ai + bi
        odd[g] = (dr * c - di * s, di * c + dr * s)
    out = [None] * n
    out[0::2], out[1::2] = real_inverse(even), real_inverse(odd)
    return out


def complex_short(x, direction):
    n = len(x)
    if n == 1:
        return x
    even, odd = complex_short(x[0::2], direction), complex_short(x[1::2], direction)
    out = [None] * n
    for k in range(n // 2):
        o_r, o_i = odd[k]
        if k == 0:
            wr, wi = o_r, o_i
        elif 4 * k == n:
            wr, wi = -direction * o_i, direction * o_r
        else:
            c = math.cos(2 * math.pi * k / n)
            s = direction * math.sin(2 * math.pi * k / n)
            wr, wi = o_r * c - o_i * s, o_i * c + o_r * s
        er, ei = even[k]
        out[k] = (er + wr, ei + wi)
        out[k + n // 2] = (er - wr, ei - wi)
    return out


def split(x):
    high = x.astype(jnp.bfloat16)
    return high, (x - high.astype(F32)).astype(jnp.bfloat16)


def dot(a, b):
    return jnp.dot(a, b, preferred_element_type=F32)


def dot_right(x, table):
    high, low = split(x)
    return dot(high, table[0]) + (dot(low, table[0]) + dot(high, table[1]))


def dot_left(table, x):
    high, low = split(x)
    return dot(table[0], high) + (dot(table[0], low) + dot(table[1], high))


def forward_kernel(x_ref, table_ref, first_ref, cos_ref, sin_ref, out_ref, held):
    owners, rows, width = x_ref.shape
    slots = held.shape[0]
    per = width // WIDE

    @pl.loop(0, rows // 8)
    def _(tile):
        at = pl.ds(pl.multiple_of(tile * 8, 8), 8)
        for lane in range(0, WIDE, LANES):
            x = [
                x_ref[j, at, pl.ds(b * WIDE + lane, LANES)]
                for j in range(owners)
                for b in range(per)
            ]
            g = real_forward(x)
            held[0, at, pl.ds(lane, LANES)] = g[0][0]
            held[0, at, pl.ds(WIDE + lane, LANES)] = g[slots][0]
            for k in range(1, slots):
                c = cos_ref[pl.ds(k, 1), pl.ds(lane, LANES)]
                s = sin_ref[pl.ds(k, 1), pl.ds(lane, LANES)]
                re, im = g[k]
                held[k, at, pl.ds(lane, LANES)] = re * c + im * s
                held[k, at, pl.ds(WIDE + lane, LANES)] = im * c - re * s

    group = min(8, slots)

    @pl.loop(0, slots // group)
    def _(step):
        at = pl.ds(step * group, group)
        x = held[at].reshape(group * rows, 2 * WIDE)
        y = dot_right(x, table_ref).reshape(group, rows, 2 * WIDE)
        out_ref[at, 0] = y[:, :, :WIDE]
        out_ref[at, 1] = y[:, :, WIDE:]

    y = dot_right(held[0], first_ref)
    out_ref[0, 0] = y[:, :WIDE]
    out_ref[0, 1] = y[:, WIDE:]


def inverse_kernel(x_ref, table_ref, first_ref, cos_ref, sin_ref, out_ref, held):
    owners, rows, width = out_ref.shape
    slots = held.shape[0]
    per = width // WIDE
    group = min(8, slots)

    @pl.loop(0, slots // group)
    def _(step):
        at = pl.ds(step * group, group)
        x = jnp.concatenate([x_ref[at, 0], x_ref[at, 1]], axis=-1)
        y = dot_right(x.reshape(group * rows, 2 * WIDE), table_ref)
        held[at] = y.reshape(group, rows, 2 * WIDE)

    held[0] = dot_right(jnp.concatenate([x_ref[0, 0], x_ref[0, 1]], axis=-1), first_ref)

    @pl.loop(0, rows // 8)
    def _(tile):
        at = pl.ds(pl.multiple_of(tile * 8, 8), 8)
        for lane in range(0, WIDE, LANES):
            v = [(held[0, at, pl.ds(lane, LANES)], None)]
            for k in range(1, slots):
                c = cos_ref[pl.ds(k, 1), pl.ds(lane, LANES)]
                s = sin_ref[pl.ds(k, 1), pl.ds(lane, LANES)]
                re = held[k, at, pl.ds(lane, LANES)]
                im = held[k, at, pl.ds(WIDE + lane, LANES)]
                v.append((re * c - im * s, im * c + re * s))
            v.append((held[0, at, pl.ds(WIDE + lane, LANES)], None))
            y = real_inverse(v)
            for j in range(owners):
                for b in range(per):
                    place = pl.ds(b * WIDE + lane, LANES)
                    out_ref[j, at, place] = y[j * per + b]


def whole(shape):
    return pl.BlockSpec(shape, lambda i: (0,) * len(shape))


def params():
    return pltpu.CompilerParams(vmem_limit_bytes=56 * 2**20)


def channel_forward(x):
    owners, rows, width = x.shape
    channels = owners * width
    slots = channels // WIDE // 2
    block = min(32, rows)
    table, first, cos, sin = channel_tables(channels)
    tables = [jnp.asarray(halves(table)), jnp.asarray(halves(first)), jnp.asarray(cos), jnp.asarray(sin)]
    return pl.pallas_call(
        forward_kernel,
        grid=(rows // block,),
        in_specs=[pl.BlockSpec((owners, block, width), lambda i: (0, i, 0))]
        + [whole(t.shape) for t in tables],
        out_specs=pl.BlockSpec((slots, 2, block, WIDE), lambda i: (0, 0, i, 0)),
        out_shape=jax.ShapeDtypeStruct((slots, 2, rows, WIDE), F32),
        scratch_shapes=[pltpu.VMEM((slots, block, 2 * WIDE), F32)],
        compiler_params=params(),
        name="channel_forward",
    )(x, *tables)


def channel_inverse(x, owners):
    slots, _, rows, _ = x.shape
    channels = 2 * slots * WIDE
    width = channels // owners
    block = min(32, rows)
    table, first, cos, sin = channel_tables(channels)
    tables = [jnp.asarray(halves(table.T)), jnp.asarray(halves(first.T)), jnp.asarray(cos), jnp.asarray(sin)]
    return pl.pallas_call(
        inverse_kernel,
        grid=(rows // block,),
        in_specs=[pl.BlockSpec((slots, 2, block, WIDE), lambda i: (0, 0, i, 0))]
        + [whole(t.shape) for t in tables],
        out_specs=pl.BlockSpec((owners, block, width), lambda i: (0, i, 0)),
        out_shape=jax.ShapeDtypeStruct((owners, rows, width), F32),
        scratch_shapes=[pltpu.VMEM((slots, block, 2 * WIDE), F32)],
        compiler_params=params(),
        name="channel_inverse",
    )(x, *tables)


def others(devices, visit):
    spread = math.gcd(4, devices)

    @pl.loop(1, devices)
    def _(i):
        visit(lax.rem(i, spread) * (devices // spread) + i // spread)


def greet(devices, owners, me):
    barrier = pltpu.get_barrier_semaphore()

    def hail(step):
        to = lax.rem(me + step, devices)
        pl.semaphore_signal(
            barrier, inc=1, device_id=(to // owners, lax.rem(to, owners)),
            device_id_type=pl.DeviceIdType.MESH,
        )

    others(devices, hail)
    pl.semaphore_wait(barrier, devices - 1)


def send_out_kernel(
    x_ref, table_ref, first_ref, cos_ref, sin_ref, out_ref,
    got, held, ready, own_in, own_out, chan_send, chan_recv, full_send, full_recv,
):
    owners, rows, _ = x_ref.shape
    chunks, devices, _, block, _ = ready.shape
    line, place = lax.axis_index("tm"), lax.axis_index("chan")
    me = line * owners + place

    def part(q):
        return pl.ds(pl.multiple_of(q * block, block), block)

    def across(q, step, back=False):
        to = lax.rem(place + step, owners)
        source = lax.rem(place + owners - step, owners) if back else place
        return pltpu.make_async_remote_copy(
            src_ref=x_ref.at[to, part(q)], dst_ref=got.at[source, part(q)],
            send_sem=chan_send.at[q, step], recv_sem=chan_recv.at[q, step],
            device_id=(line, to), device_id_type=pl.DeviceIdType.MESH,
        )

    def everywhere(q, step, back=False):
        to = lax.rem(me + step, devices)
        source = lax.rem(me + devices - step, devices) if back else me
        return pltpu.make_async_remote_copy(
            src_ref=ready.at[q, to], dst_ref=out_ref.at[source, :, part(q)],
            send_sem=full_send.at[q, step], recv_sem=full_recv.at[q, step],
            device_id=(to // owners, lax.rem(to, owners)), device_id_type=pl.DeviceIdType.MESH,
        )

    def take_own(q):
        return pltpu.make_async_copy(x_ref.at[place, part(q)], got.at[place, part(q)], own_in.at[q])

    def give_own(q):
        return pltpu.make_async_copy(ready.at[q, me], out_ref.at[me, :, part(q)], own_out.at[q])

    def begin(q):
        take_own(q).start()
        for step in range(1, owners):
            across(q, step).start()

    greet(devices, owners, me)
    ahead = min(2, chunks)
    for q in range(ahead):
        begin(q)

    @pl.loop(0, chunks)
    def _(q):
        take_own(q).wait()
        for step in range(1, owners):
            across(q, step, True).wait_recv()

        @pl.when(q + ahead < chunks)
        def _():
            begin(q + ahead)

        forward_kernel(
            got.at[:, part(q)], table_ref, first_ref, cos_ref, sin_ref, ready.at[q], held
        )
        give_own(q).start()
        others(devices, lambda step: everywhere(q, step).start())

    @pl.loop(0, chunks)
    def _(q):
        for step in range(1, owners):
            across(q, step).wait_send()
        give_own(q).wait()

        def finish(step):
            everywhere(q, step).wait_send()
            everywhere(q, step, True).wait_recv()

        others(devices, finish)


def send_back_kernel(
    x_ref, turn_ref, cos_t_ref, sin_t_ref, factor_ref, fir_ref,
    table_ref, first_ref, cos_ref, sin_ref, out_ref,
    lanes, line_held, padded, got, held, ready,
    own_in, own_half, own_part, own_out, half_send, half_recv,
    chan_send, chan_recv, full_send, full_recv,
):
    owners, rows, _ = out_ref.shape
    devices = x_ref.shape[0]
    chunks = own_part.shape[0]
    block = rows // chunks
    line, place = lax.axis_index("tm"), lax.axis_index("chan")
    me = line * owners + place
    first_half, second_half = pl.ds(0, LANES), pl.ds(LANES, LANES)

    def part(q):
        return pl.ds(pl.multiple_of(q * block, block), block)

    def across(q, step, back=False):
        to = lax.rem(place + step, owners)
        source = lax.rem(place + owners - step, owners) if back else place
        return pltpu.make_async_remote_copy(
            src_ref=ready.at[to, part(q)], dst_ref=out_ref.at[source, part(q)],
            send_sem=chan_send.at[q, step], recv_sem=chan_recv.at[q, step],
            device_id=(line, to), device_id_type=pl.DeviceIdType.MESH,
        )

    def half(step, back=False):
        to = lax.rem(me + step, devices)
        source = lax.rem(me + devices - step, devices) if back else me
        return pltpu.make_async_remote_copy(
            src_ref=lanes.at[0, to], dst_ref=got.at[source, :, :, first_half],
            send_sem=half_send.at[step], recv_sem=half_recv.at[step],
            device_id=(to // owners, lax.rem(to, owners)), device_id_type=pl.DeviceIdType.MESH,
        )

    def everywhere(q, step, back=False):
        to = lax.rem(me + step, devices)
        source = lax.rem(me + devices - step, devices) if back else me
        return pltpu.make_async_remote_copy(
            src_ref=lanes.at[1, to, :, part(q)], dst_ref=got.at[source, :, part(q), second_half],
            send_sem=full_send.at[q, step], recv_sem=full_recv.at[q, step],
            device_id=(to // owners, lax.rem(to, owners)), device_id_type=pl.DeviceIdType.MESH,
        )

    def take_own(side):
        return pltpu.make_async_copy(
            x_ref.at[:, :, :, pl.ds(side * LANES, LANES)], lanes.at[side], own_in.at[side]
        )

    def keep_half():
        return pltpu.make_async_copy(lanes.at[0, me], got.at[me, :, :, first_half], own_half)

    def keep_part(q):
        return pltpu.make_async_copy(
            lanes.at[1, me, :, part(q)], got.at[me, :, part(q), second_half], own_part.at[q]
        )

    def give_own(q):
        return pltpu.make_async_copy(ready.at[place, part(q)], out_ref.at[place, part(q)], own_out.at[q])

    def begin(q):
        keep_part(q).start()
        others(devices, lambda step: everywhere(q, step).start())

    def transform(side):
        time_kernel(
            lanes.at[side], turn_ref, cos_t_ref, sin_t_ref,
            factor_ref.at[:, :, pl.ds(side * LANES, LANES)], fir_ref, lanes.at[side],
            line_held, padded,
        )

    take_own(0).start()
    take_own(1).start()
    greet(devices, owners, me)
    take_own(0).wait()
    transform(0)
    keep_half().start()
    others(devices, lambda step: half(step).start())
    take_own(1).wait()
    transform(1)
    ahead = min(2, chunks)
    for q in range(ahead):
        begin(q)
    keep_half().wait()
    others(devices, lambda step: half(step, True).wait_recv())

    @pl.loop(0, chunks)
    def _(q):
        keep_part(q).wait()
        others(devices, lambda step: everywhere(q, step, True).wait_recv())

        @pl.when(q + ahead < chunks)
        def _():
            begin(q + ahead)

        inverse_kernel(
            got.at[:, :, part(q)], table_ref, first_ref, cos_ref, sin_ref,
            ready.at[:, part(q)], held,
        )
        give_own(q).start()
        for step in range(1, owners):
            across(q, step).start()

    others(devices, lambda step: half(step).wait_send())

    @pl.loop(0, chunks)
    def _(q):
        others(devices, lambda step: everywhere(q, step).wait_send())
        give_own(q).wait()
        for step in range(1, owners):
            across(q, step).wait_send()
            across(q, step, True).wait_recv()


CHUNK_OUT = 16
CHUNK_BACK = 32


def exchange_semaphores(chunks, owners, devices):
    dma = pltpu.SemaphoreType.DMA
    return [
        dma((chunks,)), dma((chunks,)), dma((chunks, owners)), dma((chunks, owners)),
        dma((chunks, devices)), dma((chunks, devices)),
    ]


def exchange_call(kernel, ident, operands, out_shape, scratch):
    anywhere = pl.BlockSpec(memory_space=pl.ANY)
    inside = pl.BlockSpec(memory_space=pltpu.VMEM)
    return pl.pallas_call(
        kernel,
        in_specs=[anywhere] + [inside] * (len(operands) - 1),
        out_specs=anywhere,
        out_shape=jax.ShapeDtypeStruct(out_shape, F32),
        scratch_shapes=scratch,
        compiler_params=pltpu.CompilerParams(
            vmem_limit_bytes=56 * 2**20, collective_id=ident, has_side_effects=True
        ),
        name=kernel.__name__,
    )(*operands)


def send_out(x, devices):
    owners, rows, width = x.shape
    channels = owners * width
    slots = channels // WIDE // 2
    block = min(CHUNK_OUT, rows)
    chunks = rows // block
    table, first, cos, sin = channel_tables(channels)
    operands = [x] + [jnp.asarray(t) for t in (halves(table), halves(first), cos, sin)]
    buffers = [(owners, rows, width), (slots, block, 2 * WIDE), (chunks, slots, 2, block, WIDE)]
    scratch = [pltpu.VMEM(b, F32) for b in buffers] + exchange_semaphores(chunks, owners, devices)
    return exchange_call(send_out_kernel, 0, operands, (devices, 2, rows, WIDE), scratch)


def send_back(x, factor, taps, owners):
    slots, _, rows, _ = x.shape
    channels = 2 * slots * WIDE
    width = channels // owners
    block = min(CHUNK_BACK, rows)
    chunks = rows // block
    table, first, cos, sin = channel_tables(channels)
    operands = [x, *time_tables(slots * rows), factor, fir_table(taps)]
    operands += [jnp.asarray(t) for t in (halves(table.T), halves(first.T), cos, sin)]
    samples = slots * rows
    buffers = [
        (2, slots, 2, rows, LANES), (2, samples // WIDE, WIDE, LANES),
        (2, samples + 2 * LANES, LANES), x.shape, (slots, block, 2 * WIDE), (owners, rows, width),
    ]
    dma = pltpu.SemaphoreType.DMA
    scratch = [pltpu.VMEM(b, F32) for b in buffers]
    scratch += [dma((2,)), dma(()), dma((chunks,)), dma((chunks,)), dma((slots,)), dma((slots,))]
    scratch += exchange_semaphores(chunks, owners, slots)[2:]
    return exchange_call(send_back_kernel, 1, operands, (owners, rows, width), scratch)


def time_kernel(x_ref, table_ref, cos_ref, sin_ref, factor_ref, fir_ref, out_ref, held, line):
    devices, _, rows, lanes = x_ref.shape
    radix = held.shape[1]
    per = WIDE // rows

    for part in range(per):
        @pl.loop(0, rows // 8)
        def _(tile):
            at = pl.ds(pl.multiple_of(tile * 8, 8), 8)
            to = pl.ds(pl.multiple_of(part * rows + tile * 8, 8), 8)
            x = [(x_ref[b * per + part, 0, at], x_ref[b * per + part, 1, at]) for b in range(radix)]
            y = complex_short(x, -1.0)
            for g in range(radix):
                re, im = y[g]
                c, s = cos_ref[g, to], sin_ref[g, to]
                held[0, g, to] = re * c + im * s
                held[1, g, to] = im * c - re * s

    @pl.loop(0, radix)
    def _(g):
        y = dot_left(table_ref, jnp.concatenate([held[0, g], held[1, g]], axis=1))
        factor = factor_ref[g]
        re = (y[:WIDE, :lanes] + y[WIDE:, lanes:]) * factor
        im = (y[:WIDE, lanes:] - y[WIDE:, :lanes]) * factor
        y = dot_left(table_ref, jnp.concatenate([re, im], axis=1))
        re = y[:WIDE, :lanes] - y[WIDE:, lanes:]
        im = y[:WIDE, lanes:] + y[WIDE:, :lanes]
        c, s = cos_ref[g], sin_ref[g]
        held[0, g] = re * c - im * s
        held[1, g] = im * c + re * s

    edge = line.shape[1] - LANES
    for part in range(2):
        line[part, :LANES] = jnp.zeros((LANES, lanes), F32)
        line[part, edge:] = jnp.zeros((LANES, lanes), F32)

    @pl.loop(0, WIDE // 8)
    def _(tile):
        at = pl.ds(pl.multiple_of(tile * 8, 8), 8)
        y = complex_short([(held[0, g, at], held[1, g, at]) for g in range(radix)], 1.0)
        for b in range(radix):
            to = pl.ds(pl.multiple_of(LANES + b * WIDE + tile * 8, 8), 8)
            line[0, to] = y[b][0]
            line[1, to] = y[b][1]

    @pl.loop(0, radix)
    def _(b):
        at = pl.ds(pl.multiple_of(b * WIDE, WIDE), 2 * WIDE)
        y = dot_left(fir_ref, jnp.concatenate([line[0, at], line[1, at]], axis=1))
        to = pl.ds(b * per, per)
        out_ref[to, 0] = y[:, :lanes].reshape(per, rows, lanes)
        out_ref[to, 1] = y[:, lanes:].reshape(per, rows, lanes)


def fir_table(taps):
    count = taps.shape[0]
    shift = LANES - (count - 1) // 2
    period = 2 * WIDE + 1
    row = jnp.pad(taps, (shift, period - count - shift))
    table = jnp.tile(row, WIDE)[: WIDE * 2 * WIDE].reshape(WIDE, 2 * WIDE)
    high = lax.reduce_precision(table, 8, 7)
    return jnp.stack([high, table - high]).astype(jnp.bfloat16)


def time_tables(samples):
    radix = samples // WIDE
    a = np.arange(WIDE)
    cos, sin = turn(a[:, None] * a[None, :], WIDE)
    table = jnp.asarray(halves(np.concatenate([cos, sin], axis=0)))
    spread = (radix, WIDE, LANES)
    turns = turn(np.arange(radix)[:, None] * a[None, :], samples)
    return [table] + [
        jnp.asarray(np.broadcast_to(t.astype(np.float32)[:, :, None], spread)) for t in turns
    ]


def time_stage(x, factor, taps):
    devices, _, rows, piece = x.shape
    samples = devices * rows
    radix = samples // WIDE
    table, *turns = time_tables(samples)
    fir = fir_table(taps)
    block = pl.BlockSpec((devices, 2, rows, LANES), lambda i: (0, 0, 0, i))
    return pl.pallas_call(
        time_kernel,
        grid=(piece // LANES,),
        in_specs=[
            block,
            whole(table.shape),
            whole(turns[0].shape),
            whole(turns[1].shape),
            pl.BlockSpec((radix, WIDE, LANES), lambda i: (0, 0, i)),
            whole(fir.shape),
        ],
        out_specs=block,
        out_shape=jax.ShapeDtypeStruct(x.shape, F32),
        scratch_shapes=[
            pltpu.VMEM((2, radix, WIDE, LANES), F32),
            pltpu.VMEM((2, samples + 2 * LANES, LANES), F32),
        ],
        compiler_params=params(),
        name="time_stage",
    )(x, table, *turns, factor, fir)


def mask_factor(band_edges, channels, piece, width):
    samples = band_edges.shape[1]
    owner = lax.axis_index("tm") * lax.axis_size("chan") + lax.axis_index("chan")
    order = jnp.asarray(wave_order(channels))
    wave = lax.dynamic_slice_in_dim(order, owner * piece, piece)
    wave = jnp.pad(wave, (0, width - piece))[None, None, :]
    edges = band_edges.reshape(2, WIDE, samples // WIDE).transpose(0, 2, 1)[:, :, :, None]
    kept = (wave >= edges[0]) & (wave <= edges[1])
    weight = jnp.where(wave == 0, 1.0, 2.0).astype(F32)
    return jnp.where(kept, weight, 0.0) / float(samples * channels)


def regroup(x, devices):
    slots, _, rows, _ = x.shape
    share = devices // slots
    if share == 1:
        return x
    x = x.reshape(slots, 2, rows, share, WIDE // share).transpose(0, 3, 1, 2, 4)
    return x.reshape(devices, 2, rows, WIDE // share)


def ungroup(x, slots):
    devices, _, rows, piece = x.shape
    share = devices // slots
    if share == 1:
        return x
    x = x.reshape(slots, share, 2, rows, piece).transpose(0, 2, 3, 1, 4)
    return x.reshape(slots, 2, rows, WIDE)


def exchange(x, axes):
    return lax.all_to_all(x, axes, split_axis=0, concat_axis=0, tiled=True)


def per_device(traces, band_edges, taps, gain_table, gain_index):
    owners = lax.axis_size("chan")
    devices = lax.axis_size("tm") * owners
    length, width = traces.shape
    channels = owners * width
    slots = channels // WIDE // 2
    piece = channels // 2 // devices
    padded = max(piece, LANES)
    matches = gain_index[:, None] == jnp.arange(gain_table.shape[0], dtype=jnp.int32)[None, :]
    gains = jnp.sum(jnp.where(matches, gain_table[None, :], 0.0), axis=1)
    factor = mask_factor(band_edges, channels, piece, padded)

    if devices == slots:
        spectra = send_out(traces.reshape(owners, length // owners, width), devices)
        local = send_back(spectra, factor, taps, owners)
        return local.reshape(length, width) * gains[None, :]

    gathered = exchange(traces.reshape(owners, length // owners, width), "chan")
    spectra = exchange(regroup(channel_forward(gathered), devices), AXES)
    if padded > piece:
        spectra = jnp.pad(spectra, ((0, 0), (0, 0), (0, 0), (0, padded - piece)))
    spectra = time_stage(spectra, factor, taps)
    if padded > piece:
        spectra = spectra[..., :piece]
    returned = ungroup(exchange(spectra, AXES), slots)
    local = exchange(channel_inverse(returned, owners), "chan")
    return local.reshape(length, width) * gains[None, :]


def solution(mesh):
    in_specs = (P("tm", "chan"), P(), P(), P(), P("chan"))
    out_specs = P("tm", "chan")
    return jax.shard_map(
        per_device, mesh=mesh, in_specs=in_specs, out_specs=out_specs, check_vma=False
    )
```

```python
import functools
import math

import jax
import jax.numpy as jnp
import ml_dtypes
import numpy as np
from jax import lax
from jax.experimental import pallas as pl
from jax.experimental.pallas import tpu as pltpu
from jax.sharding import PartitionSpec as P

WIDE = 256
LANES = 128
AXES = ("tm", "chan")
F32 = jnp.float32


def halves(table):
    table = np.asarray(table, np.float32)
    high = table.astype(ml_dtypes.bfloat16)
    low = (table - high.astype(np.float32)).astype(ml_dtypes.bfloat16)
    return np.stack([high, low])


def turn(product, period):
    theta = (product % period) * (2.0 * math.pi / period)
    return np.cos(theta), np.sin(theta)


def channel_tables(channels):
    radix = channels // WIDE
    a = np.arange(WIDE)
    cos, sin = turn(a[:, None] * a[None, :], WIDE)
    sign = np.where(a < WIDE // 2, 1.0, -1.0)
    table = np.block([[cos, -sin * sign], [sin, cos * sign]])
    low = np.arange(WIDE // 2)
    cos_0, sin_0 = turn(a[:, None] * low[None, :], WIDE)
    cos_m, sin_m = turn(a[:, None] * (radix // 2 + radix * low)[None, :], channels)
    none = np.zeros_like(cos_0)
    first = np.block([[cos_0, none, -sin_0, none], [none, cos_m, none, -sin_m]])
    cos_t, sin_t = turn(np.arange(radix // 2)[:, None] * a[None, :], channels)
    return table, first, cos_t.astype(np.float32), sin_t.astype(np.float32)


def wave_order(channels):
    radix = channels // WIDE
    h = np.arange(WIDE)
    low = np.arange(WIDE // 2)
    rows = [np.concatenate([radix * low, radix // 2 + radix * low])]
    for g in range(1, radix // 2):
        wave = g + radix * h
        rows.append(np.where(h < WIDE // 2, wave, channels - wave))
    return np.concatenate(rows).astype(np.int32)


def real_forward(x):
    n = len(x)
    if n == 2:
        return [(x[0] + x[1], None), (x[0] - x[1], None)]
    even, odd = real_forward(x[0::2]), real_forward(x[1::2])
    out = [None] * (n // 2 + 1)
    out[0] = (even[0][0] + odd[0][0], None)
    out[n // 2] = (even[0][0] - odd[0][0], None)
    out[n // 4] = (even[n // 4][0], -odd[n // 4][0])
    for k in range(1, n // 4):
        c, s = math.cos(2 * math.pi * k / n), math.sin(2 * math.pi * k / n)
        er, ei = even[k]
        o_r, o_i = odd[k]
        wr, wi = o_r * c + o_i * s, o_i * c - o_r * s
        out[k] = (er + wr, ei + wi)
        out[n // 2 - k] = (er - wr, wi - ei)
    return out


def real_inverse(v):
    n = 2 * (len(v) - 1)
    if n == 2:
        return [v[0][0] + v[1][0], v[0][0] - v[1][0]]
    q = n // 4
    even, odd = [None] * (q + 1), [None] * (q + 1)
    even[0] = (v[0][0] + v[n // 2][0], None)
    odd[0] = (v[0][0] - v[n // 2][0], None)
    even[q] = (v[q][0], None)
    odd[q] = (-v[q][1], None)
    for g in range(1, q):
        c, s = math.cos(2 * math.pi * g / n), math.sin(2 * math.pi * g / n)
        ar, ai = v[g]
        br, bi = v[n // 2 - g]
        even[g] = (ar + br, ai - bi)
        dr, di = ar - br, ai + bi
        odd[g] = (dr * c - di * s, di * c + dr * s)
    out = [None] * n
    out[0::2], out[1::2] = real_inverse(even), real_inverse(odd)
    return out


def complex_short(x, direction):
    n = len(x)
    if n == 1:
        return x
    even, odd = complex_short(x[0::2], direction), complex_short(x[1::2], direction)
    out = [None] * n
    for k in range(n // 2):
        o_r, o_i = odd[k]
        if k == 0:
            wr, wi = o_r, o_i
        elif 4 * k == n:
            wr, wi = -direction * o_i, direction * o_r
        else:
            c = math.cos(2 * math.pi * k / n)
            s = direction * math.sin(2 * math.pi * k / n)
            wr, wi = o_r * c - o_i * s, o_i * c + o_r * s
        er, ei = even[k]
        out[k] = (er + wr, ei + wi)
        out[k + n // 2] = (er - wr, ei - wi)
    return out


def split(x):
    high = x.astype(jnp.bfloat16)
    return high, (x - high.astype(F32)).astype(jnp.bfloat16)


def dot(a, b):
    return jnp.dot(a, b, preferred_element_type=F32)


def dot_right(x, table):
    high, low = split(x)
    return dot(high, table[0]) + (dot(low, table[0]) + dot(high, table[1]))


def dot_left(table, x):
    high, low = split(x)
    return dot(table[0], high) + (dot(table[0], low) + dot(table[1], high))


def forward_kernel(x_ref, table_ref, first_ref, cos_ref, sin_ref, out_ref, held):
    owners, rows, width = x_ref.shape
    slots = held.shape[0]
    per = width // WIDE

    @pl.loop(0, rows // 8)
    def _(tile):
        at = pl.ds(pl.multiple_of(tile * 8, 8), 8)
        for lane in range(0, WIDE, LANES):
            x = [
                x_ref[j, at, pl.ds(b * WIDE + lane, LANES)]
                for j in range(owners)
                for b in range(per)
            ]
            g = real_forward(x)
            held[0, at, pl.ds(lane, LANES)] = g[0][0]
            held[0, at, pl.ds(WIDE + lane, LANES)] = g[slots][0]
            for k in range(1, slots):
                c = cos_ref[pl.ds(k, 1), pl.ds(lane, LANES)]
                s = sin_ref[pl.ds(k, 1), pl.ds(lane, LANES)]
                re, im = g[k]
                held[k, at, pl.ds(lane, LANES)] = re * c + im * s
                held[k, at, pl.ds(WIDE + lane, LANES)] = im * c - re * s

    group = min(8, slots)

    @pl.loop(0, slots // group)
    def _(step):
        at = pl.ds(step * group, group)
        x = held[at].reshape(group * rows, 2 * WIDE)
        y = dot_right(x, table_ref).reshape(group, rows, 2 * WIDE)
        out_ref[at, 0] = y[:, :, :WIDE]
        out_ref[at, 1] = y[:, :, WIDE:]

    y = dot_right(held[0], first_ref)
    out_ref[0, 0] = y[:, :WIDE]
    out_ref[0, 1] = y[:, WIDE:]


def inverse_kernel(x_ref, *refs):
    inverse_body(lambda at: jnp.concatenate([x_ref[at, 0], x_ref[at, 1]], axis=-1), *refs)


def inverse_body(load, table_ref, first_ref, cos_ref, sin_ref, out_ref, held):
    owners, rows, width = out_ref.shape
    slots = held.shape[0]
    per = width // WIDE
    group = min(8, slots)

    @pl.loop(0, slots // group)
    def _(step):
        at = pl.ds(step * group, group)
        y = dot_right(load(at).reshape(group * rows, 2 * WIDE), table_ref)
        held[at] = y.reshape(group, rows, 2 * WIDE)

    held[0] = dot_right(load(0), first_ref)

    @pl.loop(0, rows // 8)
    def _(tile):
        at = pl.ds(pl.multiple_of(tile * 8, 8), 8)
        for lane in range(0, WIDE, LANES):
            v = [(held[0, at, pl.ds(lane, LANES)], None)]
            for k in range(1, slots):
                c = cos_ref[pl.ds(k, 1), pl.ds(lane, LANES)]
                s = sin_ref[pl.ds(k, 1), pl.ds(lane, LANES)]
                re = held[k, at, pl.ds(lane, LANES)]
                im = held[k, at, pl.ds(WIDE + lane, LANES)]
                v.append((re * c - im * s, im * c + re * s))
            v.append((held[0, at, pl.ds(WIDE + lane, LANES)], None))
            y = real_inverse(v)
            for j in range(owners):
                for b in range(per):
                    place = pl.ds(b * WIDE + lane, LANES)
                    out_ref[j, at, place] = y[j * per + b]


def whole(shape):
    return pl.BlockSpec(shape, lambda i: (0,) * len(shape))


def params():
    return pltpu.CompilerParams(vmem_limit_bytes=56 * 2**20)


def channel_forward(x):
    owners, rows, width = x.shape
    channels = owners * width
    slots = channels // WIDE // 2
    block = min(32, rows)
    table, first, cos, sin = channel_tables(channels)
    tables = [jnp.asarray(halves(table)), jnp.asarray(halves(first)), jnp.asarray(cos), jnp.asarray(sin)]
    return pl.pallas_call(
        forward_kernel,
        grid=(rows // block,),
        in_specs=[pl.BlockSpec((owners, block, width), lambda i: (0, i, 0))]
        + [whole(t.shape) for t in tables],
        out_specs=pl.BlockSpec((slots, 2, block, WIDE), lambda i: (0, 0, i, 0)),
        out_shape=jax.ShapeDtypeStruct((slots, 2, rows, WIDE), F32),
        scratch_shapes=[pltpu.VMEM((slots, block, 2 * WIDE), F32)],
        compiler_params=params(),
        name="channel_forward",
    )(x, *tables)


def channel_inverse(x, owners):
    slots, _, rows, _ = x.shape
    channels = 2 * slots * WIDE
    width = channels // owners
    block = min(32, rows)
    table, first, cos, sin = channel_tables(channels)
    tables = [jnp.asarray(halves(table.T)), jnp.asarray(halves(first.T)), jnp.asarray(cos), jnp.asarray(sin)]
    return pl.pallas_call(
        inverse_kernel,
        grid=(rows // block,),
        in_specs=[pl.BlockSpec((slots, 2, block, WIDE), lambda i: (0, 0, i, 0))]
        + [whole(t.shape) for t in tables],
        out_specs=pl.BlockSpec((owners, block, width), lambda i: (0, i, 0)),
        out_shape=jax.ShapeDtypeStruct((owners, rows, width), F32),
        scratch_shapes=[pltpu.VMEM((slots, block, 2 * WIDE), F32)],
        compiler_params=params(),
        name="channel_inverse",
    )(x, *tables)


def others(devices, visit):
    spread = math.gcd(4, devices)

    @pl.loop(1, devices)
    def _(i):
        visit(lax.rem(i, spread) * (devices // spread) + i // spread)


def greet(devices, owners, me):
    barrier = pltpu.get_barrier_semaphore()

    def hail(step):
        to = lax.rem(me + step, devices)
        pl.semaphore_signal(
            barrier, inc=1, device_id=(to // owners, lax.rem(to, owners)),
            device_id_type=pl.DeviceIdType.MESH,
        )

    others(devices, hail)
    pl.semaphore_wait(barrier, devices - 1)


def send_out_kernel(
    x_ref, table_ref, first_ref, cos_ref, sin_ref, out_ref,
    got, held, ready, own_in, own_out, chan_send, chan_recv, full_send, full_recv,
):
    owners, rows, _ = x_ref.shape
    chunks, devices, _, block, _ = ready.shape
    line, place = lax.axis_index("tm"), lax.axis_index("chan")
    me = line * owners + place

    def part(q):
        return pl.ds(pl.multiple_of(q * block, block), block)

    def across(q, step, back=False):
        to = lax.rem(place + step, owners)
        source = lax.rem(place + owners - step, owners) if back else place
        return pltpu.make_async_remote_copy(
            src_ref=x_ref.at[to, part(q)], dst_ref=got.at[source, part(q)],
            send_sem=chan_send.at[q, step], recv_sem=chan_recv.at[q, step],
            device_id=(line, to), device_id_type=pl.DeviceIdType.MESH,
        )

    def everywhere(q, step, back=False):
        to = lax.rem(me + step, devices)
        source = lax.rem(me + devices - step, devices) if back else me
        return pltpu.make_async_remote_copy(
            src_ref=ready.at[q, to], dst_ref=out_ref.at[source * chunks + q],
            send_sem=full_send.at[q, step], recv_sem=full_recv.at[q, step],
            device_id=(to // owners, lax.rem(to, owners)), device_id_type=pl.DeviceIdType.MESH,
        )

    def take_own(q):
        return pltpu.make_async_copy(x_ref.at[place, part(q)], got.at[place, part(q)], own_in.at[q])

    def give_own(q):
        return pltpu.make_async_copy(ready.at[q, me], out_ref.at[me * chunks + q], own_out.at[q])

    def begin(q):
        take_own(q).start()
        for step in range(1, owners):
            across(q, step).start()

    greet(devices, owners, me)
    ahead = min(2, chunks)
    for q in range(ahead):
        begin(q)

    @pl.loop(0, chunks)
    def _(q):
        take_own(q).wait()
        for step in range(1, owners):
            across(q, step, True).wait_recv()

        @pl.when(q + ahead < chunks)
        def _():
            begin(q + ahead)

        forward_kernel(
            got.at[:, part(q)], table_ref, first_ref, cos_ref, sin_ref, ready.at[q], held
        )
        give_own(q).start()
        others(devices, lambda step: everywhere(q, step).start())

    @pl.loop(0, chunks)
    def _(q):
        for step in range(1, owners):
            across(q, step).wait_send()
        give_own(q).wait()

        def finish(step):
            everywhere(q, step).wait_send()
            everywhere(q, step, True).wait_recv()

        others(devices, finish)


def send_back_kernel(
    x_ref, turn_ref, cos_t_ref, sin_t_ref, factor_ref, fir_ref,
    table_ref, first_ref, cos_ref, sin_ref, out_ref,
    lanes, line_held, padded, got, held, ready,
    own_in, own_half, own_part, own_out, half_send, half_recv,
    chan_send, chan_recv, full_send, full_recv,
):
    owners, rows, _ = out_ref.shape
    _, devices, chunks, _, _, _ = got.shape
    block = rows // chunks
    line, place = lax.axis_index("tm"), lax.axis_index("chan")
    me = line * owners + place

    def run(device):
        return pl.ds(device * chunks, chunks)

    def part(q):
        return pl.ds(pl.multiple_of(q * block, block), block)

    def across(q, step, back=False):
        to = lax.rem(place + step, owners)
        source = lax.rem(place + owners - step, owners) if back else place
        return pltpu.make_async_remote_copy(
            src_ref=ready.at[to, part(q)], dst_ref=out_ref.at[source, part(q)],
            send_sem=chan_send.at[q, step], recv_sem=chan_recv.at[q, step],
            device_id=(line, to), device_id_type=pl.DeviceIdType.MESH,
        )

    def half(step, back=False):
        to = lax.rem(me + step, devices)
        source = lax.rem(me + devices - step, devices) if back else me
        return pltpu.make_async_remote_copy(
            src_ref=lanes.at[0, run(to)], dst_ref=got.at[0, source],
            send_sem=half_send.at[step], recv_sem=half_recv.at[step],
            device_id=(to // owners, lax.rem(to, owners)), device_id_type=pl.DeviceIdType.MESH,
        )

    def everywhere(q, step, back=False):
        to = lax.rem(me + step, devices)
        source = lax.rem(me + devices - step, devices) if back else me
        return pltpu.make_async_remote_copy(
            src_ref=lanes.at[1, to * chunks + q], dst_ref=got.at[1, source, q],
            send_sem=full_send.at[q, step], recv_sem=full_recv.at[q, step],
            device_id=(to // owners, lax.rem(to, owners)), device_id_type=pl.DeviceIdType.MESH,
        )

    def take_own(side):
        return pltpu.make_async_copy(
            x_ref.at[:, :, :, pl.ds(side * LANES, LANES)], lanes.at[side], own_in.at[side]
        )

    def keep_half():
        return pltpu.make_async_copy(lanes.at[0, run(me)], got.at[0, me], own_half)

    def keep_part(q):
        return pltpu.make_async_copy(
            lanes.at[1, me * chunks + q], got.at[1, me, q], own_part.at[q]
        )

    def give_own(q):
        return pltpu.make_async_copy(ready.at[place, part(q)], out_ref.at[place, part(q)], own_out.at[q])

    def begin(q):
        keep_part(q).start()
        others(devices, lambda step: everywhere(q, step).start())

    def transform(side):
        time_kernel(
            lanes.at[side], turn_ref, cos_t_ref, sin_t_ref,
            factor_ref.at[:, :, pl.ds(side * LANES, LANES)], fir_ref, lanes.at[side],
            line_held, padded,
        )

    take_own(0).start()
    take_own(1).start()
    greet(devices, owners, me)
    take_own(0).wait()
    transform(0)
    keep_half().start()
    others(devices, lambda step: half(step).start())
    take_own(1).wait()
    transform(1)
    ahead = min(2, chunks)
    for q in range(ahead):
        begin(q)
    keep_half().wait()
    others(devices, lambda step: half(step, True).wait_recv())

    @pl.loop(0, chunks)
    def _(q):
        keep_part(q).wait()
        others(devices, lambda step: everywhere(q, step, True).wait_recv())

        @pl.when(q + ahead < chunks)
        def _():
            begin(q + ahead)

        def load(at):
            return jnp.concatenate([got[side, at, q, p] for p in range(2) for side in range(2)], axis=-1)

        inverse_body(
            load, table_ref, first_ref, cos_ref, sin_ref,
            ready.at[:, part(q)], held,
        )
        give_own(q).start()
        for step in range(1, owners):
            across(q, step).start()

    others(devices, lambda step: half(step).wait_send())

    @pl.loop(0, chunks)
    def _(q):
        others(devices, lambda step: everywhere(q, step).wait_send())
        give_own(q).wait()
        for step in range(1, owners):
            across(q, step).wait_send()
            across(q, step, True).wait_recv()


CHUNK = 16


def exchange_semaphores(chunks, owners, devices):
    dma = pltpu.SemaphoreType.DMA
    return [
        dma((chunks,)), dma((chunks,)), dma((chunks, owners)), dma((chunks, owners)),
        dma((chunks, devices)), dma((chunks, devices)),
    ]


def exchange_call(kernel, ident, operands, out_shape, scratch):
    anywhere = pl.BlockSpec(memory_space=pl.ANY)
    inside = pl.BlockSpec(memory_space=pltpu.VMEM)
    return pl.pallas_call(
        kernel,
        in_specs=[anywhere] + [inside] * (len(operands) - 1),
        out_specs=anywhere,
        out_shape=jax.ShapeDtypeStruct(out_shape, F32),
        scratch_shapes=scratch,
        compiler_params=pltpu.CompilerParams(
            vmem_limit_bytes=56 * 2**20, collective_id=ident, has_side_effects=True
        ),
        name=kernel.__name__,
    )(*operands)


def send_out(x, devices):
    owners, rows, width = x.shape
    channels = owners * width
    slots = channels // WIDE // 2
    block = min(CHUNK, rows)
    chunks = rows // block
    table, first, cos, sin = channel_tables(channels)
    operands = [x] + [jnp.asarray(t) for t in (halves(table), halves(first), cos, sin)]
    buffers = [(owners, rows, width), (slots, block, 2 * WIDE), (chunks, slots, 2, block, WIDE)]
    scratch = [pltpu.VMEM(b, F32) for b in buffers] + exchange_semaphores(chunks, owners, devices)
    return exchange_call(send_out_kernel, 0, operands, (devices * chunks, 2, block, WIDE), scratch)


def send_back(x, factor, taps, owners, devices, channels):
    pieces, _, block, _ = x.shape
    samples = pieces * block
    slots = channels // WIDE // 2
    chunks = pieces // devices
    rows = chunks * block
    table, first, cos, sin = channel_tables(channels)
    operands = [x, *time_tables(samples), factor, fir_table(taps)]
    operands += [jnp.asarray(t) for t in (halves(table.T), halves(first.T), cos, sin)]
    shape = (owners, rows, channels // owners)
    buffers = [
        (2, pieces, 2, block, LANES), (2, samples // WIDE, WIDE, LANES),
        (2, samples + 2 * LANES, LANES), (2, devices, chunks, 2, block, LANES),
        (slots, block, 2 * WIDE), shape,
    ]
    dma = pltpu.SemaphoreType.DMA
    scratch = [pltpu.VMEM(b, F32) for b in buffers]
    scratch += [dma((2,)), dma(()), dma((chunks,)), dma((chunks,)), dma((devices,)), dma((devices,))]
    scratch += exchange_semaphores(chunks, owners, devices)[2:]
    return exchange_call(send_back_kernel, 1, operands, shape, scratch)


def time_kernel(x_ref, table_ref, cos_ref, sin_ref, factor_ref, fir_ref, out_ref, held, line):
    devices, _, rows, lanes = x_ref.shape
    radix = held.shape[1]
    per = WIDE // rows

    @pl.loop(0, WIDE // 8)
    def _(tile):
        part = tile // (rows // 8)
        at = pl.ds(pl.multiple_of(lax.rem(tile, rows // 8) * 8, 8), 8)
        to = pl.ds(pl.multiple_of(tile * 8, 8), 8)
        x = [(x_ref[b * per + part, 0, at], x_ref[b * per + part, 1, at]) for b in range(radix)]
        y = complex_short(x, -1.0)
        for g in range(radix):
            re, im = y[g]
            c, s = cos_ref[g, to], sin_ref[g, to]
            held[0, g, to] = re * c + im * s
            held[1, g, to] = im * c - re * s

    @pl.loop(0, radix)
    def _(g):
        y = dot_left(table_ref, jnp.concatenate([held[0, g], held[1, g]], axis=1))
        factor = factor_ref[g]
        re = (y[:WIDE, :lanes] + y[WIDE:, lanes:]) * factor
        im = (y[:WIDE, lanes:] - y[WIDE:, :lanes]) * factor
        y = dot_left(table_ref, jnp.concatenate([re, im], axis=1))
        re = y[:WIDE, :lanes] - y[WIDE:, lanes:]
        im = y[:WIDE, lanes:] + y[WIDE:, :lanes]
        c, s = cos_ref[g], sin_ref[g]
        held[0, g] = re * c - im * s
        held[1, g] = im * c + re * s

    edge = line.shape[1] - LANES
    for part in range(2):
        line[part, :LANES] = jnp.zeros((LANES, lanes), F32)
        line[part, edge:] = jnp.zeros((LANES, lanes), F32)

    @pl.loop(0, WIDE // 8)
    def _(tile):
        at = pl.ds(pl.multiple_of(tile * 8, 8), 8)
        y = complex_short([(held[0, g, at], held[1, g, at]) for g in range(radix)], 1.0)
        for b in range(radix):
            to = pl.ds(pl.multiple_of(LANES + b * WIDE + tile * 8, 8), 8)
            line[0, to] = y[b][0]
            line[1, to] = y[b][1]

    @pl.loop(0, radix)
    def _(b):
        at = pl.ds(pl.multiple_of(b * WIDE, WIDE), 2 * WIDE)
        y = dot_left(fir_ref, jnp.concatenate([line[0, at], line[1, at]], axis=1))
        to = pl.ds(b * per, per)
        out_ref[to, 0] = y[:, :lanes].reshape(per, rows, lanes)
        out_ref[to, 1] = y[:, lanes:].reshape(per, rows, lanes)


def fir_table(taps):
    count = taps.shape[0]
    shift = LANES - (count - 1) // 2
    period = 2 * WIDE + 1
    row = jnp.pad(taps, (shift, period - count - shift))
    table = jnp.tile(row, WIDE)[: WIDE * 2 * WIDE].reshape(WIDE, 2 * WIDE)
    high = lax.reduce_precision(table, 8, 7)
    return jnp.stack([high, table - high]).astype(jnp.bfloat16)


def time_tables(samples):
    radix = samples // WIDE
    a = np.arange(WIDE)
    cos, sin = turn(a[:, None] * a[None, :], WIDE)
    table = jnp.asarray(halves(np.concatenate([cos, sin], axis=0)))
    spread = (radix, WIDE, LANES)
    turns = turn(np.arange(radix)[:, None] * a[None, :], samples)
    return [table] + [
        jnp.asarray(np.broadcast_to(t.astype(np.float32)[:, :, None], spread)) for t in turns
    ]


def time_stage(x, factor, taps):
    devices, _, rows, piece = x.shape
    samples = devices * rows
    radix = samples // WIDE
    table, *turns = time_tables(samples)
    fir = fir_table(taps)
    block = pl.BlockSpec((devices, 2, rows, LANES), lambda i: (0, 0, 0, i))
    return pl.pallas_call(
        time_kernel,
        grid=(piece // LANES,),
        in_specs=[
            block,
            whole(table.shape),
            whole(turns[0].shape),
            whole(turns[1].shape),
            pl.BlockSpec((radix, WIDE, LANES), lambda i: (0, 0, i)),
            whole(fir.shape),
        ],
        out_specs=block,
        out_shape=jax.ShapeDtypeStruct(x.shape, F32),
        scratch_shapes=[
            pltpu.VMEM((2, radix, WIDE, LANES), F32),
            pltpu.VMEM((2, samples + 2 * LANES, LANES), F32),
        ],
        compiler_params=params(),
        name="time_stage",
    )(x, table, *turns, factor, fir)


def mask_factor(band_edges, channels, piece, width):
    samples = band_edges.shape[1]
    owner = lax.axis_index("tm") * lax.axis_size("chan") + lax.axis_index("chan")
    order = jnp.asarray(wave_order(channels))
    wave = lax.dynamic_slice_in_dim(order, owner * piece, piece)
    wave = jnp.pad(wave, (0, width - piece))[None, None, :]
    edges = band_edges.reshape(2, WIDE, samples // WIDE).transpose(0, 2, 1)[:, :, :, None]
    kept = (wave >= edges[0]) & (wave <= edges[1])
    weight = jnp.where(wave == 0, 1.0, 2.0).astype(F32)
    return jnp.where(kept, weight, 0.0) / float(samples * channels)


def regroup(x, devices):
    slots, _, rows, _ = x.shape
    share = devices // slots
    if share == 1:
        return x
    x = x.reshape(slots, 2, rows, share, WIDE // share).transpose(0, 3, 1, 2, 4)
    return x.reshape(devices, 2, rows, WIDE // share)


def ungroup(x, slots):
    devices, _, rows, piece = x.shape
    share = devices // slots
    if share == 1:
        return x
    x = x.reshape(slots, share, 2, rows, piece).transpose(0, 2, 3, 1, 4)
    return x.reshape(slots, 2, rows, WIDE)


def exchange(x, axes):
    return lax.all_to_all(x, axes, split_axis=0, concat_axis=0, tiled=True)


def per_device(traces, band_edges, taps, gain_table, gain_index):
    owners = lax.axis_size("chan")
    devices = lax.axis_size("tm") * owners
    length, width = traces.shape
    channels = owners * width
    slots = channels // WIDE // 2
    piece = channels // 2 // devices
    padded = max(piece, LANES)
    matches = gain_index[:, None] == jnp.arange(gain_table.shape[0], dtype=jnp.int32)[None, :]
    gains = jnp.sum(jnp.where(matches, gain_table[None, :], 0.0), axis=1)
    factor = mask_factor(band_edges, channels, piece, padded)

    if devices == slots:
        spectra = send_out(traces.reshape(owners, length // owners, width), devices)
        local = send_back(spectra, factor, taps, owners, devices, channels)
        return local.reshape(length, width) * gains[None, :]

    gathered = exchange(traces.reshape(owners, length // owners, width), "chan")
    spectra = exchange(regroup(channel_forward(gathered), devices), AXES)
    if padded > piece:
        spectra = jnp.pad(spectra, ((0, 0), (0, 0), (0, 0), (0, padded - piece)))
    spectra = time_stage(spectra, factor, taps)
    if padded > piece:
        spectra = spectra[..., :piece]
    returned = ungroup(exchange(spectra, AXES), slots)
    local = exchange(channel_inverse(returned, owners), "chan")
    return local.reshape(length, width) * gains[None, :]


def solution(mesh):
    in_specs = (P("tm", "chan"), P(), P(), P(), P("chan"))
    out_specs = P("tm", "chan")
    return jax.shard_map(
        per_device, mesh=mesh, in_specs=in_specs, out_specs=out_specs, check_vma=False
    )
```

```python
import functools
import math

import jax
import jax.numpy as jnp
import ml_dtypes
import numpy as np
from jax import lax
from jax.experimental import pallas as pl
from jax.experimental.pallas import tpu as pltpu
from jax.sharding import PartitionSpec as P

WIDE = 256
LANES = 128
AXES = ("tm", "chan")
F32 = jnp.float32


def halves(table, axis):
    table = np.asarray(table, np.float32)
    high = table.astype(ml_dtypes.bfloat16)
    low = (table - high.astype(np.float32)).astype(ml_dtypes.bfloat16)
    return np.concatenate([high, low, high], axis=axis)


def turn(product, period):
    theta = (product % period) * (2.0 * math.pi / period)
    return np.cos(theta), np.sin(theta)


def channel_tables(channels):
    radix = channels // WIDE
    a = np.arange(WIDE)
    cos, sin = turn(a[:, None] * a[None, :], WIDE)
    sign = np.where(a < WIDE // 2, 1.0, -1.0)
    table = np.block([[cos, -sin * sign], [sin, cos * sign]])
    low = np.arange(WIDE // 2)
    cos_0, sin_0 = turn(a[:, None] * low[None, :], WIDE)
    cos_m, sin_m = turn(a[:, None] * (radix // 2 + radix * low)[None, :], channels)
    none = np.zeros_like(cos_0)
    first = np.block([[cos_0, none, -sin_0, none], [none, cos_m, none, -sin_m]])
    cos_t, sin_t = turn(np.arange(radix // 2)[:, None] * a[None, :], channels)
    return table, first, cos_t.astype(np.float32), sin_t.astype(np.float32)


def wave_order(channels):
    radix = channels // WIDE
    h = np.arange(WIDE)
    low = np.arange(WIDE // 2)
    rows = [np.concatenate([radix * low, radix // 2 + radix * low])]
    for g in range(1, radix // 2):
        wave = g + radix * h
        rows.append(np.where(h < WIDE // 2, wave, channels - wave))
    return np.concatenate(rows).astype(np.int32)


def real_forward(x):
    n = len(x)
    if n == 2:
        return [(x[0] + x[1], None), (x[0] - x[1], None)]
    even, odd = real_forward(x[0::2]), real_forward(x[1::2])
    out = [None] * (n // 2 + 1)
    out[0] = (even[0][0] + odd[0][0], None)
    out[n // 2] = (even[0][0] - odd[0][0], None)
    out[n // 4] = (even[n // 4][0], -odd[n // 4][0])
    for k in range(1, n // 4):
        c, s = math.cos(2 * math.pi * k / n), math.sin(2 * math.pi * k / n)
        er, ei = even[k]
        o_r, o_i = odd[k]
        wr, wi = o_r * c + o_i * s, o_i * c - o_r * s
        out[k] = (er + wr, ei + wi)
        out[n // 2 - k] = (er - wr, wi - ei)
    return out


def real_inverse(v):
    n = 2 * (len(v) - 1)
    if n == 2:
        return [v[0][0] + v[1][0], v[0][0] - v[1][0]]
    q = n // 4
    even, odd = [None] * (q + 1), [None] * (q + 1)
    even[0] = (v[0][0] + v[n // 2][0], None)
    odd[0] = (v[0][0] - v[n // 2][0], None)
    even[q] = (v[q][0], None)
    odd[q] = (-v[q][1], None)
    for g in range(1, q):
        c, s = math.cos(2 * math.pi * g / n), math.sin(2 * math.pi * g / n)
        ar, ai = v[g]
        br, bi = v[n // 2 - g]
        even[g] = (ar + br, ai - bi)
        dr, di = ar - br, ai + bi
        odd[g] = (dr * c - di * s, di * c + dr * s)
    out = [None] * n
    out[0::2], out[1::2] = real_inverse(even), real_inverse(odd)
    return out


def complex_short(x, direction):
    n = len(x)
    if n == 1:
        return x
    even, odd = complex_short(x[0::2], direction), complex_short(x[1::2], direction)
    out = [None] * n
    for k in range(n // 2):
        o_r, o_i = odd[k]
        if k == 0:
            wr, wi = o_r, o_i
        elif 4 * k == n:
            wr, wi = -direction * o_i, direction * o_r
        else:
            c = math.cos(2 * math.pi * k / n)
            s = direction * math.sin(2 * math.pi * k / n)
            wr, wi = o_r * c - o_i * s, o_i * c + o_r * s
        er, ei = even[k]
        out[k] = (er + wr, ei + wi)
        out[k + n // 2] = (er - wr, ei - wi)
    return out


def split(x, axis):
    high = x.astype(jnp.bfloat16)
    low = (x - high.astype(F32)).astype(jnp.bfloat16)
    return jnp.concatenate([high, high, low], axis=axis)


def dot_right(x, table_ref):
    return jnp.dot(split(x, 1), table_ref[...], preferred_element_type=F32)


def dot_left(table_ref, x):
    return jnp.dot(table_ref[...], split(x, 0), preferred_element_type=F32)


def forward_kernel(x_ref, table_ref, first_ref, cos_ref, sin_ref, out_ref, held):
    owners, rows, width = x_ref.shape
    slots = held.shape[0]
    per = width // WIDE

    @pl.loop(0, rows // 8)
    def _(tile):
        at = pl.ds(pl.multiple_of(tile * 8, 8), 8)
        for lane in range(0, WIDE, LANES):
            x = [
                x_ref[j, at, pl.ds(b * WIDE + lane, LANES)]
                for j in range(owners)
                for b in range(per)
            ]
            g = real_forward(x)
            held[0, at, pl.ds(lane, LANES)] = g[0][0]
            held[0, at, pl.ds(WIDE + lane, LANES)] = g[slots][0]
            for k in range(1, slots):
                c = cos_ref[pl.ds(k, 1), pl.ds(lane, LANES)]
                s = sin_ref[pl.ds(k, 1), pl.ds(lane, LANES)]
                re, im = g[k]
                held[k, at, pl.ds(lane, LANES)] = re * c + im * s
                held[k, at, pl.ds(WIDE + lane, LANES)] = im * c - re * s

    group = min(8, slots)

    @pl.loop(0, slots // group)
    def _(step):
        at = pl.ds(step * group, group)
        x = held[at].reshape(group * rows, 2 * WIDE)
        y = dot_right(x, table_ref).reshape(group, rows, 2 * WIDE)
        out_ref[at, 0] = y[:, :, :WIDE]
        out_ref[at, 1] = y[:, :, WIDE:]

    y = dot_right(held[0], first_ref)
    out_ref[0, 0] = y[:, :WIDE]
    out_ref[0, 1] = y[:, WIDE:]


def inverse_kernel(x_ref, *refs):
    inverse_body(lambda at: jnp.concatenate([x_ref[at, 0], x_ref[at, 1]], axis=-1), *refs)


def inverse_body(load, table_ref, first_ref, cos_ref, sin_ref, out_ref, held):
    owners, rows, width = out_ref.shape
    slots = held.shape[0]
    per = width // WIDE
    group = min(8, slots)

    @pl.loop(0, slots // group)
    def _(step):
        at = pl.ds(step * group, group)
        y = dot_right(load(at).reshape(group * rows, 2 * WIDE), table_ref)
        held[at] = y.reshape(group, rows, 2 * WIDE)

    held[0] = dot_right(load(0), first_ref)

    @pl.loop(0, rows // 8)
    def _(tile):
        at = pl.ds(pl.multiple_of(tile * 8, 8), 8)
        for lane in range(0, WIDE, LANES):
            v = [(held[0, at, pl.ds(lane, LANES)], None)]
            for k in range(1, slots):
                c = cos_ref[pl.ds(k, 1), pl.ds(lane, LANES)]
                s = sin_ref[pl.ds(k, 1), pl.ds(lane, LANES)]
                re = held[k, at, pl.ds(lane, LANES)]
                im = held[k, at, pl.ds(WIDE + lane, LANES)]
                v.append((re * c - im * s, im * c + re * s))
            v.append((held[0, at, pl.ds(WIDE + lane, LANES)], None))
            y = real_inverse(v)
            for j in range(owners):
                for b in range(per):
                    place = pl.ds(b * WIDE + lane, LANES)
                    out_ref[j, at, place] = y[j * per + b]


def whole(shape):
    return pl.BlockSpec(shape, lambda i: (0,) * len(shape))


def params():
    return pltpu.CompilerParams(vmem_limit_bytes=56 * 2**20)


def channel_forward(x):
    owners, rows, width = x.shape
    channels = owners * width
    slots = channels // WIDE // 2
    block = min(32, rows)
    table, first, cos, sin = channel_tables(channels)
    tables = [jnp.asarray(halves(table, 0)), jnp.asarray(halves(first, 0)), jnp.asarray(cos), jnp.asarray(sin)]
    return pl.pallas_call(
        forward_kernel,
        grid=(rows // block,),
        in_specs=[pl.BlockSpec((owners, block, width), lambda i: (0, i, 0))]
        + [whole(t.shape) for t in tables],
        out_specs=pl.BlockSpec((slots, 2, block, WIDE), lambda i: (0, 0, i, 0)),
        out_shape=jax.ShapeDtypeStruct((slots, 2, rows, WIDE), F32),
        scratch_shapes=[pltpu.VMEM((slots, block, 2 * WIDE), F32)],
        compiler_params=params(),
        name="channel_forward",
    )(x, *tables)


def channel_inverse(x, owners):
    slots, _, rows, _ = x.shape
    channels = 2 * slots * WIDE
    width = channels // owners
    block = min(32, rows)
    table, first, cos, sin = channel_tables(channels)
    tables = [jnp.asarray(halves(table.T, 0)), jnp.asarray(halves(first.T, 0)), jnp.asarray(cos), jnp.asarray(sin)]
    return pl.pallas_call(
        inverse_kernel,
        grid=(rows // block,),
        in_specs=[pl.BlockSpec((slots, 2, block, WIDE), lambda i: (0, 0, i, 0))]
        + [whole(t.shape) for t in tables],
        out_specs=pl.BlockSpec((owners, block, width), lambda i: (0, i, 0)),
        out_shape=jax.ShapeDtypeStruct((owners, rows, width), F32),
        scratch_shapes=[pltpu.VMEM((slots, block, 2 * WIDE), F32)],
        compiler_params=params(),
        name="channel_inverse",
    )(x, *tables)


def distance(i, devices):
    spread = math.gcd(4, devices)
    return lax.rem(i, spread) * (devices // spread) + i // spread


def others(devices, visit):
    @pl.loop(1, devices)
    def _(i):
        visit(distance(i, devices))


def greet(devices, owners, me):
    barrier = pltpu.get_barrier_semaphore()

    def hail(step):
        to = lax.rem(me + step, devices)
        pl.semaphore_signal(
            barrier, inc=1, device_id=(to // owners, lax.rem(to, owners)),
            device_id_type=pl.DeviceIdType.MESH,
        )

    others(devices, hail)
    pl.semaphore_wait(barrier, devices - 1)


def send_out_kernel(
    x_ref, table_ref, first_ref, cos_ref, sin_ref, out_ref,
    got, held, ready, own_in, own_out, chan_send, chan_recv, full_send, full_recv,
):
    owners, rows, _ = x_ref.shape
    chunks, devices, _, block, _ = ready.shape
    line, place = lax.axis_index("tm"), lax.axis_index("chan")
    me = line * owners + place

    def part(q):
        return pl.ds(pl.multiple_of(q * block, block), block)

    def across(q, step, back=False):
        to = lax.rem(place + step, owners)
        source = lax.rem(place + owners - step, owners) if back else place
        return pltpu.make_async_remote_copy(
            src_ref=x_ref.at[to, part(q)], dst_ref=got.at[source, part(q)],
            send_sem=chan_send.at[q, step], recv_sem=chan_recv.at[q, step],
            device_id=(line, to), device_id_type=pl.DeviceIdType.MESH,
        )

    def everywhere(q, step, back=False):
        to = lax.rem(me + step, devices)
        source = lax.rem(me + devices - step, devices) if back else me
        return pltpu.make_async_remote_copy(
            src_ref=ready.at[q, to], dst_ref=out_ref.at[source * chunks + q],
            send_sem=full_send.at[q, step], recv_sem=full_recv.at[q, step],
            device_id=(to // owners, lax.rem(to, owners)), device_id_type=pl.DeviceIdType.MESH,
        )

    def take_own(q):
        return pltpu.make_async_copy(x_ref.at[place, part(q)], got.at[place, part(q)], own_in.at[q])

    def give_own(q):
        return pltpu.make_async_copy(ready.at[q, me], out_ref.at[me * chunks + q], own_out.at[q])

    def begin(q):
        take_own(q).start()
        for step in range(1, owners):
            across(q, step).start()

    greet(devices, owners, me)
    ahead = min(2, chunks)
    for q in range(ahead):
        begin(q)

    @pl.loop(0, chunks)
    def _(q):
        take_own(q).wait()
        for step in range(1, owners):
            across(q, step, True).wait_recv()

        @pl.when(q + ahead < chunks)
        def _():
            begin(q + ahead)

        forward_kernel(
            got.at[:, part(q)], table_ref, first_ref, cos_ref, sin_ref, ready.at[q], held
        )
        give_own(q).start()
        others(devices, lambda step: everywhere(q, step).start())

    @pl.loop(0, chunks)
    def _(q):
        for step in range(1, owners):
            across(q, step).wait_send()
        give_own(q).wait()

        def finish(step):
            everywhere(q, step).wait_send()
            everywhere(q, step, True).wait_recv()

        others(devices, finish)


def send_back_kernel(
    x_ref, turn_ref, cos_t_ref, sin_t_ref, factor_ref, fir_ref,
    table_ref, first_ref, cos_ref, sin_ref, out_ref,
    lanes, line_held, padded, got, held, ready,
    own_in, own_half, own_part, own_out, half_send, half_recv,
    chan_send, chan_recv, full_send, full_recv,
):
    owners, rows, _ = out_ref.shape
    _, devices, chunks, _, _, _ = got.shape
    block = rows // chunks
    line, place = lax.axis_index("tm"), lax.axis_index("chan")
    me = line * owners + place

    def run(device):
        return pl.ds(device * chunks, chunks)

    def part(q):
        return pl.ds(pl.multiple_of(q * block, block), block)

    def across(q, step, back=False):
        to = lax.rem(place + step, owners)
        source = lax.rem(place + owners - step, owners) if back else place
        return pltpu.make_async_remote_copy(
            src_ref=ready.at[to, part(q)], dst_ref=out_ref.at[source, part(q)],
            send_sem=chan_send.at[q, step], recv_sem=chan_recv.at[q, step],
            device_id=(line, to), device_id_type=pl.DeviceIdType.MESH,
        )

    def half(step, back=False):
        to = lax.rem(me + step, devices)
        source = lax.rem(me + devices - step, devices) if back else me
        return pltpu.make_async_remote_copy(
            src_ref=lanes.at[0, run(to)], dst_ref=got.at[0, source],
            send_sem=half_send.at[step], recv_sem=half_recv.at[step],
            device_id=(to // owners, lax.rem(to, owners)), device_id_type=pl.DeviceIdType.MESH,
        )

    def everywhere(q, step, back=False):
        to = lax.rem(me + step, devices)
        source = lax.rem(me + devices - step, devices) if back else me
        return pltpu.make_async_remote_copy(
            src_ref=lanes.at[1, to * chunks + q], dst_ref=got.at[1, source, q],
            send_sem=full_send.at[q, step], recv_sem=full_recv.at[q, step],
            device_id=(to // owners, lax.rem(to, owners)), device_id_type=pl.DeviceIdType.MESH,
        )

    def take_own(side):
        return pltpu.make_async_copy(
            x_ref.at[:, :, :, pl.ds(side * LANES, LANES)], lanes.at[side], own_in.at[side]
        )

    def keep_half():
        return pltpu.make_async_copy(lanes.at[0, run(me)], got.at[0, me], own_half)

    def keep_part(q):
        return pltpu.make_async_copy(
            lanes.at[1, me * chunks + q], got.at[1, me, q], own_part.at[q]
        )

    def give_own(q):
        return pltpu.make_async_copy(ready.at[place, part(q)], out_ref.at[place, part(q)], own_out.at[q])

    def begin(q):
        keep_part(q).start()
        others(devices, lambda step: everywhere(q, step).start())

    def some_halves(turn_at, turns):
        share = -(-devices // turns)
        for r in range(share):
            i = turn_at * share + r

            @pl.when((i > 0) & (i < devices))
            def _():
                half(distance(i, devices)).start()

    def transform(side, between=None):
        time_kernel(
            lanes.at[side], turn_ref, cos_t_ref, sin_t_ref,
            factor_ref.at[:, :, pl.ds(side * LANES, LANES)], fir_ref, lanes.at[side],
            line_held, padded, between,
        )

    take_own(0).start()
    take_own(1).start()
    greet(devices, owners, me)
    take_own(0).wait()
    transform(0)
    keep_half().start()
    take_own(1).wait()
    transform(1, some_halves)
    ahead = min(4, chunks)
    for q in range(ahead):
        begin(q)
    keep_half().wait()
    others(devices, lambda step: half(step, True).wait_recv())

    @pl.loop(0, chunks)
    def _(q):
        keep_part(q).wait()
        others(devices, lambda step: everywhere(q, step, True).wait_recv())

        @pl.when(q + ahead < chunks)
        def _():
            begin(q + ahead)

        def load(at):
            return jnp.concatenate([got[side, at, q, p] for p in range(2) for side in range(2)], axis=-1)

        inverse_body(
            load, table_ref, first_ref, cos_ref, sin_ref,
            ready.at[:, part(q)], held,
        )
        give_own(q).start()
        for step in range(1, owners):
            across(q, step).start()

    others(devices, lambda step: half(step).wait_send())

    @pl.loop(0, chunks)
    def _(q):
        others(devices, lambda step: everywhere(q, step).wait_send())
        give_own(q).wait()
        for step in range(1, owners):
            across(q, step).wait_send()
            across(q, step, True).wait_recv()


CHUNK = 16


def exchange_semaphores(chunks, owners, devices):
    dma = pltpu.SemaphoreType.DMA
    return [
        dma((chunks,)), dma((chunks,)), dma((chunks, owners)), dma((chunks, owners)),
        dma((chunks, devices)), dma((chunks, devices)),
    ]


def exchange_call(kernel, ident, operands, out_shape, scratch):
    anywhere = pl.BlockSpec(memory_space=pl.ANY)
    inside = pl.BlockSpec(memory_space=pltpu.VMEM)
    return pl.pallas_call(
        kernel,
        in_specs=[anywhere] + [inside] * (len(operands) - 1),
        out_specs=anywhere,
        out_shape=jax.ShapeDtypeStruct(out_shape, F32),
        scratch_shapes=scratch,
        compiler_params=pltpu.CompilerParams(
            vmem_limit_bytes=56 * 2**20, collective_id=ident, has_side_effects=True
        ),
        name=kernel.__name__,
    )(*operands)


def send_out(x, devices):
    owners, rows, width = x.shape
    channels = owners * width
    slots = channels // WIDE // 2
    block = min(CHUNK, rows)
    chunks = rows // block
    table, first, cos, sin = channel_tables(channels)
    operands = [x] + [jnp.asarray(t) for t in (halves(table, 0), halves(first, 0), cos, sin)]
    buffers = [(owners, rows, width), (slots, block, 2 * WIDE), (chunks, slots, 2, block, WIDE)]
    scratch = [pltpu.VMEM(b, F32) for b in buffers] + exchange_semaphores(chunks, owners, devices)
    return exchange_call(send_out_kernel, 0, operands, (devices * chunks, 2, block, WIDE), scratch)


def send_back(x, factor, taps, owners, devices, channels):
    pieces, _, block, _ = x.shape
    samples = pieces * block
    slots = channels // WIDE // 2
    chunks = pieces // devices
    rows = chunks * block
    table, first, cos, sin = channel_tables(channels)
    operands = [x, *time_tables(samples), factor, fir_table(taps)]
    operands += [jnp.asarray(t) for t in (halves(table.T, 0), halves(first.T, 0), cos, sin)]
    shape = (owners, rows, channels // owners)
    buffers = [
        (2, pieces, 2, block, LANES), (2, samples // WIDE, WIDE, LANES),
        (2, samples + 2 * LANES, LANES), (2, devices, chunks, 2, block, LANES),
        (slots, block, 2 * WIDE), shape,
    ]
    dma = pltpu.SemaphoreType.DMA
    scratch = [pltpu.VMEM(b, F32) for b in buffers]
    scratch += [dma((2,)), dma(()), dma((chunks,)), dma((chunks,)), dma((devices,)), dma((devices,))]
    scratch += exchange_semaphores(chunks, owners, devices)[2:]
    return exchange_call(send_back_kernel, 1, operands, shape, scratch)


def time_kernel(x_ref, table_ref, cos_ref, sin_ref, factor_ref, fir_ref, out_ref, held, line, between=None):
    devices, _, rows, lanes = x_ref.shape
    radix = held.shape[1]
    per = WIDE // rows

    @pl.loop(0, WIDE // 8)
    def _(tile):
        part = tile // (rows // 8)
        at = pl.ds(pl.multiple_of(lax.rem(tile, rows // 8) * 8, 8), 8)
        to = pl.ds(pl.multiple_of(tile * 8, 8), 8)
        x = [(x_ref[b * per + part, 0, at], x_ref[b * per + part, 1, at]) for b in range(radix)]
        y = complex_short(x, -1.0)
        for g in range(radix):
            re, im = y[g]
            c, s = cos_ref[g, to], sin_ref[g, to]
            held[0, g, to] = re * c + im * s
            held[1, g, to] = im * c - re * s

    @pl.loop(0, radix)
    def _(g):
        if between is not None:
            between(g, 2 * radix)
        y = dot_left(table_ref, jnp.concatenate([held[0, g], held[1, g]], axis=1))
        factor = factor_ref[g]
        re = (y[:WIDE, :lanes] + y[WIDE:, lanes:]) * factor
        im = (y[:WIDE, lanes:] - y[WIDE:, :lanes]) * factor
        y = dot_left(table_ref, jnp.concatenate([re, im], axis=1))
        re = y[:WIDE, :lanes] - y[WIDE:, lanes:]
        im = y[:WIDE, lanes:] + y[WIDE:, :lanes]
        c, s = cos_ref[g], sin_ref[g]
        held[0, g] = re * c - im * s
        held[1, g] = im * c + re * s

    edge = line.shape[1] - LANES
    for part in range(2):
        line[part, :LANES] = jnp.zeros((LANES, lanes), F32)
        line[part, edge:] = jnp.zeros((LANES, lanes), F32)

    @pl.loop(0, WIDE // 8)
    def _(tile):
        at = pl.ds(pl.multiple_of(tile * 8, 8), 8)
        y = complex_short([(held[0, g, at], held[1, g, at]) for g in range(radix)], 1.0)
        for b in range(radix):
            to = pl.ds(pl.multiple_of(LANES + b * WIDE + tile * 8, 8), 8)
            line[0, to] = y[b][0]
            line[1, to] = y[b][1]

    @pl.loop(0, radix)
    def _(b):
        if between is not None:
            between(radix + b, 2 * radix)
        at = pl.ds(pl.multiple_of(b * WIDE, WIDE), 2 * WIDE)
        y = dot_left(fir_ref, jnp.concatenate([line[0, at], line[1, at]], axis=1))
        to = pl.ds(b * per, per)
        out_ref[to, 0] = y[:, :lanes].reshape(per, rows, lanes)
        out_ref[to, 1] = y[:, lanes:].reshape(per, rows, lanes)


def fir_table(taps):
    count = taps.shape[0]
    shift = LANES - (count - 1) // 2
    period = 2 * WIDE + 1
    row = jnp.pad(taps, (shift, period - count - shift))
    table = jnp.tile(row, WIDE)[: WIDE * 2 * WIDE].reshape(WIDE, 2 * WIDE)
    high = lax.reduce_precision(table, 8, 7)
    return jnp.concatenate([high, table - high, high], axis=1).astype(jnp.bfloat16)


def time_tables(samples):
    radix = samples // WIDE
    a = np.arange(WIDE)
    cos, sin = turn(a[:, None] * a[None, :], WIDE)
    table = jnp.asarray(halves(np.concatenate([cos, sin], axis=0), 1))
    spread = (radix, WIDE, LANES)
    turns = turn(np.arange(radix)[:, None] * a[None, :], samples)
    return [table] + [
        jnp.asarray(np.broadcast_to(t.astype(np.float32)[:, :, None], spread)) for t in turns
    ]


def time_stage(x, factor, taps):
    devices, _, rows, piece = x.shape
    samples = devices * rows
    radix = samples // WIDE
    table, *turns = time_tables(samples)
    fir = fir_table(taps)
    block = pl.BlockSpec((devices, 2, rows, LANES), lambda i: (0, 0, 0, i))
    return pl.pallas_call(
        time_kernel,
        grid=(piece // LANES,),
        in_specs=[
            block,
            whole(table.shape),
            whole(turns[0].shape),
            whole(turns[1].shape),
            pl.BlockSpec((radix, WIDE, LANES), lambda i: (0, 0, i)),
            whole(fir.shape),
        ],
        out_specs=block,
        out_shape=jax.ShapeDtypeStruct(x.shape, F32),
        scratch_shapes=[
            pltpu.VMEM((2, radix, WIDE, LANES), F32),
            pltpu.VMEM((2, samples + 2 * LANES, LANES), F32),
        ],
        compiler_params=params(),
        name="time_stage",
    )(x, table, *turns, factor, fir)


def mask_factor(band_edges, channels, piece, width):
    samples = band_edges.shape[1]
    owner = lax.axis_index("tm") * lax.axis_size("chan") + lax.axis_index("chan")
    order = jnp.asarray(wave_order(channels))
    wave = lax.dynamic_slice_in_dim(order, owner * piece, piece)
    wave = jnp.pad(wave, (0, width - piece))[None, None, :]
    edges = band_edges.reshape(2, WIDE, samples // WIDE).transpose(0, 2, 1)[:, :, :, None]
    kept = (wave >= edges[0]) & (wave <= edges[1])
    weight = jnp.where(wave == 0, 1.0, 2.0).astype(F32)
    return jnp.where(kept, weight, 0.0) / float(samples * channels)


def regroup(x, devices):
    slots, _, rows, _ = x.shape
    share = devices // slots
    if share == 1:
        return x
    x = x.reshape(slots, 2, rows, share, WIDE // share).transpose(0, 3, 1, 2, 4)
    return x.reshape(devices, 2, rows, WIDE // share)


def ungroup(x, slots):
    devices, _, rows, piece = x.shape
    share = devices // slots
    if share == 1:
        return x
    x = x.reshape(slots, share, 2, rows, piece).transpose(0, 2, 3, 1, 4)
    return x.reshape(slots, 2, rows, WIDE)


def exchange(x, axes):
    return lax.all_to_all(x, axes, split_axis=0, concat_axis=0, tiled=True)


def per_device(traces, band_edges, taps, gain_table, gain_index):
    owners = lax.axis_size("chan")
    devices = lax.axis_size("tm") * owners
    length, width = traces.shape
    channels = owners * width
    slots = channels // WIDE // 2
    piece = channels // 2 // devices
    padded = max(piece, LANES)
    matches = gain_index[:, None] == jnp.arange(gain_table.shape[0], dtype=jnp.int32)[None, :]
    gains = jnp.sum(jnp.where(matches, gain_table[None, :], 0.0), axis=1)
    factor = mask_factor(band_edges, channels, piece, padded)

    if devices == slots:
        spectra = send_out(traces.reshape(owners, length // owners, width), devices)
        local = send_back(spectra, factor, taps, owners, devices, channels)
        return local.reshape(length, width) * gains[None, :]

    gathered = exchange(traces.reshape(owners, length // owners, width), "chan")
    spectra = exchange(regroup(channel_forward(gathered), devices), AXES)
    if padded > piece:
        spectra = jnp.pad(spectra, ((0, 0), (0, 0), (0, 0), (0, padded - piece)))
    spectra = time_stage(spectra, factor, taps)
    if padded > piece:
        spectra = spectra[..., :piece]
    returned = ungroup(exchange(spectra, AXES), slots)
    local = exchange(channel_inverse(returned, owners), "chan")
    return local.reshape(length, width) * gains[None, :]


def solution(mesh):
    in_specs = (P("tm", "chan"), P(), P(), P(), P("chan"))
    out_specs = P("tm", "chan")
    return jax.shard_map(
        per_device, mesh=mesh, in_specs=in_specs, out_specs=out_specs, check_vma=False
    )
```

```python
import functools
import math

import jax
import jax.numpy as jnp
import ml_dtypes
import numpy as np
from jax import lax
from jax.experimental import pallas as pl
from jax.experimental.pallas import tpu as pltpu
from jax.sharding import PartitionSpec as P

WIDE = 256
LANES = 128
AXES = ("tm", "chan")
F32 = jnp.float32


def halves(table):
    table = np.asarray(table, np.float32)
    high = table.astype(ml_dtypes.bfloat16)
    low = (table - high.astype(np.float32)).astype(ml_dtypes.bfloat16)
    return np.stack([high, low])


def turn(product, period):
    theta = (product % period) * (2.0 * math.pi / period)
    return np.cos(theta), np.sin(theta)


def channel_tables(channels):
    radix = channels // WIDE
    a = np.arange(WIDE)
    cos, sin = turn(a[:, None] * a[None, :], WIDE)
    sign = np.where(a < WIDE // 2, 1.0, -1.0)
    table = np.block([[cos, -sin * sign], [sin, cos * sign]])
    low = np.arange(WIDE // 2)
    cos_0, sin_0 = turn(a[:, None] * low[None, :], WIDE)
    cos_m, sin_m = turn(a[:, None] * (radix // 2 + radix * low)[None, :], channels)
    none = np.zeros_like(cos_0)
    first = np.block([[cos_0, none, -sin_0, none], [none, cos_m, none, -sin_m]])
    cos_t, sin_t = turn(np.arange(radix // 2)[:, None] * a[None, :], channels)
    return table, first, cos_t.astype(np.float32), sin_t.astype(np.float32)


def wave_order(channels):
    radix = channels // WIDE
    h = np.arange(WIDE)
    low = np.arange(WIDE // 2)
    rows = [np.concatenate([radix * low, radix // 2 + radix * low])]
    for g in range(1, radix // 2):
        wave = g + radix * h
        rows.append(np.where(h < WIDE // 2, wave, channels - wave))
    return np.concatenate(rows).astype(np.int32)


def real_forward(x):
    n = len(x)
    if n == 2:
        return [(x[0] + x[1], None), (x[0] - x[1], None)]
    even, odd = real_forward(x[0::2]), real_forward(x[1::2])
    out = [None] * (n // 2 + 1)
    out[0] = (even[0][0] + odd[0][0], None)
    out[n // 2] = (even[0][0] - odd[0][0], None)
    out[n // 4] = (even[n // 4][0], -odd[n // 4][0])
    for k in range(1, n // 4):
        c, s = math.cos(2 * math.pi * k / n), math.sin(2 * math.pi * k / n)
        er, ei = even[k]
        o_r, o_i = odd[k]
        wr, wi = o_r * c + o_i * s, o_i * c - o_r * s
        out[k] = (er + wr, ei + wi)
        out[n // 2 - k] = (er - wr, wi - ei)
    return out


def real_inverse(v):
    n = 2 * (len(v) - 1)
    if n == 2:
        return [v[0][0] + v[1][0], v[0][0] - v[1][0]]
    q = n // 4
    even, odd = [None] * (q + 1), [None] * (q + 1)
    even[0] = (v[0][0] + v[n // 2][0], None)
    odd[0] = (v[0][0] - v[n // 2][0], None)
    even[q] = (v[q][0], None)
    odd[q] = (-v[q][1], None)
    for g in range(1, q):
        c, s = math.cos(2 * math.pi * g / n), math.sin(2 * math.pi * g / n)
        ar, ai = v[g]
        br, bi = v[n // 2 - g]
        even[g] = (ar + br, ai - bi)
        dr, di = ar - br, ai + bi
        odd[g] = (dr * c - di * s, di * c + dr * s)
    out = [None] * n
    out[0::2], out[1::2] = real_inverse(even), real_inverse(odd)
    return out


def complex_short(x, direction):
    n = len(x)
    if n == 1:
        return x
    even, odd = complex_short(x[0::2], direction), complex_short(x[1::2], direction)
    out = [None] * n
    for k in range(n // 2):
        o_r, o_i = odd[k]
        if k == 0:
            wr, wi = o_r, o_i
        elif 4 * k == n:
            wr, wi = -direction * o_i, direction * o_r
        else:
            c = math.cos(2 * math.pi * k / n)
            s = direction * math.sin(2 * math.pi * k / n)
            wr, wi = o_r * c - o_i * s, o_i * c + o_r * s
        er, ei = even[k]
        out[k] = (er + wr, ei + wi)
        out[k + n // 2] = (er - wr, ei - wi)
    return out


def split(x):
    high = x.astype(jnp.bfloat16)
    return high, (x - high.astype(F32)).astype(jnp.bfloat16)


def dot(a, b):
    return jnp.dot(a, b, preferred_element_type=F32)


def dot_right(x, table):
    high, low = split(x)
    return dot(high, table[0]) + (dot(low, table[0]) + dot(high, table[1]))


def dot_left(table, x):
    high, low = split(x)
    return dot(table[0], high) + (dot(table[0], low) + dot(table[1], high))


def forward_kernel(x_ref, table_ref, first_ref, cos_ref, sin_ref, out_ref, held):
    owners, rows, width = x_ref.shape
    slots = held.shape[0]
    per = width // WIDE

    @pl.loop(0, rows // 8)
    def _(tile):
        at = pl.ds(pl.multiple_of(tile * 8, 8), 8)
        for lane in range(0, WIDE, LANES):
            x = [
                x_ref[j, at, pl.ds(b * WIDE + lane, LANES)]
                for j in range(owners)
                for b in range(per)
            ]
            g = real_forward(x)
            held[0, at, pl.ds(lane, LANES)] = g[0][0]
            held[0, at, pl.ds(WIDE + lane, LANES)] = g[slots][0]
            for k in range(1, slots):
                c = cos_ref[pl.ds(k, 1), pl.ds(lane, LANES)]
                s = sin_ref[pl.ds(k, 1), pl.ds(lane, LANES)]
                re, im = g[k]
                held[k, at, pl.ds(lane, LANES)] = re * c + im * s
                held[k, at, pl.ds(WIDE + lane, LANES)] = im * c - re * s

    group = min(8, slots)

    @pl.loop(0, slots // group)
    def _(step):
        at = pl.ds(step * group, group)
        x = held[at].reshape(group * rows, 2 * WIDE)
        y = dot_right(x, table_ref).reshape(group, rows, 2 * WIDE)
        out_ref[at, 0] = y[:, :, :WIDE]
        out_ref[at, 1] = y[:, :, WIDE:]

    y = dot_right(held[0], first_ref)
    out_ref[0, 0] = y[:, :WIDE]
    out_ref[0, 1] = y[:, WIDE:]


def inverse_kernel(x_ref, *refs):
    inverse_body(lambda at: jnp.concatenate([x_ref[at, 0], x_ref[at, 1]], axis=-1), *refs)


def inverse_body(load, table_ref, first_ref, cos_ref, sin_ref, out_ref, held):
    owners, rows, width = out_ref.shape
    slots = held.shape[0]
    per = width // WIDE
    group = min(8, slots)

    @pl.loop(0, slots // group)
    def _(step):
        at = pl.ds(step * group, group)
        y = dot_right(load(at).reshape(group * rows, 2 * WIDE), table_ref)
        held[at] = y.reshape(group, rows, 2 * WIDE)

    held[0] = dot_right(load(0), first_ref)

    @pl.loop(0, rows // 8)
    def _(tile):
        at = pl.ds(pl.multiple_of(tile * 8, 8), 8)
        for lane in range(0, WIDE, LANES):
            v = [(held[0, at, pl.ds(lane, LANES)], None)]
            for k in range(1, slots):
                c = cos_ref[pl.ds(k, 1), pl.ds(lane, LANES)]
                s = sin_ref[pl.ds(k, 1), pl.ds(lane, LANES)]
                re = held[k, at, pl.ds(lane, LANES)]
                im = held[k, at, pl.ds(WIDE + lane, LANES)]
                v.append((re * c - im * s, im * c + re * s))
            v.append((held[0, at, pl.ds(WIDE + lane, LANES)], None))
            y = real_inverse(v)
            for j in range(owners):
                for b in range(per):
                    place = pl.ds(b * WIDE + lane, LANES)
                    out_ref[j, at, place] = y[j * per + b]


def whole(shape):
    return pl.BlockSpec(shape, lambda i: (0,) * len(shape))


def params():
    return pltpu.CompilerParams(vmem_limit_bytes=56 * 2**20)


def channel_forward(x):
    owners, rows, width = x.shape
    channels = owners * width
    slots = channels // WIDE // 2
    block = min(32, rows)
    table, first, cos, sin = channel_tables(channels)
    tables = [jnp.asarray(halves(table)), jnp.asarray(halves(first)), jnp.asarray(cos), jnp.asarray(sin)]
    return pl.pallas_call(
        forward_kernel,
        grid=(rows // block,),
        in_specs=[pl.BlockSpec((owners, block, width), lambda i: (0, i, 0))]
        + [whole(t.shape) for t in tables],
        out_specs=pl.BlockSpec((slots, 2, block, WIDE), lambda i: (0, 0, i, 0)),
        out_shape=jax.ShapeDtypeStruct((slots, 2, rows, WIDE), F32),
        scratch_shapes=[pltpu.VMEM((slots, block, 2 * WIDE), F32)],
        compiler_params=params(),
        name="channel_forward",
    )(x, *tables)


def channel_inverse(x, owners):
    slots, _, rows, _ = x.shape
    channels = 2 * slots * WIDE
    width = channels // owners
    block = min(32, rows)
    table, first, cos, sin = channel_tables(channels)
    tables = [jnp.asarray(halves(table.T)), jnp.asarray(halves(first.T)), jnp.asarray(cos), jnp.asarray(sin)]
    return pl.pallas_call(
        inverse_kernel,
        grid=(rows // block,),
        in_specs=[pl.BlockSpec((slots, 2, block, WIDE), lambda i: (0, 0, i, 0))]
        + [whole(t.shape) for t in tables],
        out_specs=pl.BlockSpec((owners, block, width), lambda i: (0, i, 0)),
        out_shape=jax.ShapeDtypeStruct((owners, rows, width), F32),
        scratch_shapes=[pltpu.VMEM((slots, block, 2 * WIDE), F32)],
        compiler_params=params(),
        name="channel_inverse",
    )(x, *tables)


def others(devices, visit):
    spread = math.gcd(4, devices)

    @pl.loop(1, devices)
    def _(i):
        visit(lax.rem(i, spread) * (devices // spread) + i // spread)


def greet(devices, owners, me):
    barrier = pltpu.get_barrier_semaphore()

    def hail(step):
        to = lax.rem(me + step, devices)
        pl.semaphore_signal(
            barrier, inc=1, device_id=(to // owners, lax.rem(to, owners)),
            device_id_type=pl.DeviceIdType.MESH,
        )

    others(devices, hail)
    pl.semaphore_wait(barrier, devices - 1)


def send_out_kernel(
    x_ref, table_ref, first_ref, cos_ref, sin_ref, out_ref,
    got, held, ready, own_in, own_out, chan_send, chan_recv, full_send, full_recv,
):
    owners, rows, _ = x_ref.shape
    chunks, devices, _, block, _ = ready.shape
    line, place = lax.axis_index("tm"), lax.axis_index("chan")
    me = line * owners + place

    def part(q):
        return pl.ds(pl.multiple_of(q * block, block), block)

    def across(q, step, back=False):
        to = lax.rem(place + step, owners)
        source = lax.rem(place + owners - step, owners) if back else place
        return pltpu.make_async_remote_copy(
            src_ref=x_ref.at[to, part(q)], dst_ref=got.at[source, part(q)],
            send_sem=chan_send.at[q, step], recv_sem=chan_recv.at[q, step],
            device_id=(line, to), device_id_type=pl.DeviceIdType.MESH,
        )

    def everywhere(q, step, back=False):
        to = lax.rem(me + step, devices)
        source = lax.rem(me + devices - step, devices) if back else me
        return pltpu.make_async_remote_copy(
            src_ref=ready.at[q, to], dst_ref=out_ref.at[source * chunks + q],
            send_sem=full_send.at[q, step], recv_sem=full_recv.at[q, step],
            device_id=(to // owners, lax.rem(to, owners)), device_id_type=pl.DeviceIdType.MESH,
        )

    def take_own(q):
        return pltpu.make_async_copy(x_ref.at[place, part(q)], got.at[place, part(q)], own_in.at[q])

    def give_own(q):
        return pltpu.make_async_copy(ready.at[q, me], out_ref.at[me * chunks + q], own_out.at[q])

    def begin(q):
        take_own(q).start()
        for step in range(1, owners):
            across(q, step).start()

    greet(devices, owners, me)
    ahead = min(2, chunks)
    for q in range(ahead):
        begin(q)

    @pl.loop(0, chunks)
    def _(q):
        take_own(q).wait()
        for step in range(1, owners):
            across(q, step, True).wait_recv()

        @pl.when(q + ahead < chunks)
        def _():
            begin(q + ahead)

        forward_kernel(
            got.at[:, part(q)], table_ref, first_ref, cos_ref, sin_ref, ready.at[q], held
        )
        give_own(q).start()
        others(devices, lambda step: everywhere(q, step).start())

    @pl.loop(0, chunks)
    def _(q):
        for step in range(1, owners):
            across(q, step).wait_send()
        give_own(q).wait()

        def finish(step):
            everywhere(q, step).wait_send()
            everywhere(q, step, True).wait_recv()

        others(devices, finish)


def send_back_kernel(
    x_ref, turn_ref, cos_t_ref, sin_t_ref, factor_ref, fir_ref,
    table_ref, first_ref, cos_ref, sin_ref, out_ref,
    lanes, line_held, padded, got, held, ready,
    own_in, own_half, own_part, own_out, half_send, half_recv,
    chan_send, chan_recv, full_send, full_recv,
):
    owners, rows, _ = out_ref.shape
    _, devices, chunks, _, _, _ = got.shape
    block = rows // chunks
    line, place = lax.axis_index("tm"), lax.axis_index("chan")
    me = line * owners + place

    def run(device):
        return pl.ds(device * chunks, chunks)

    def part(q):
        return pl.ds(pl.multiple_of(q * block, block), block)

    def across(q, step, back=False):
        to = lax.rem(place + step, owners)
        source = lax.rem(place + owners - step, owners) if back else place
        return pltpu.make_async_remote_copy(
            src_ref=ready.at[to, part(q)], dst_ref=out_ref.at[source, part(q)],
            send_sem=chan_send.at[q, step], recv_sem=chan_recv.at[q, step],
            device_id=(line, to), device_id_type=pl.DeviceIdType.MESH,
        )

    def half(step, back=False):
        to = lax.rem(me + step, devices)
        source = lax.rem(me + devices - step, devices) if back else me
        return pltpu.make_async_remote_copy(
            src_ref=lanes.at[0, run(to)], dst_ref=got.at[0, source],
            send_sem=half_send.at[step], recv_sem=half_recv.at[step],
            device_id=(to // owners, lax.rem(to, owners)), device_id_type=pl.DeviceIdType.MESH,
        )

    def everywhere(q, step, back=False):
        to = lax.rem(me + step, devices)
        source = lax.rem(me + devices - step, devices) if back else me
        return pltpu.make_async_remote_copy(
            src_ref=lanes.at[1, to * chunks + q], dst_ref=got.at[1, source, q],
            send_sem=full_send.at[q, step], recv_sem=full_recv.at[q, step],
            device_id=(to // owners, lax.rem(to, owners)), device_id_type=pl.DeviceIdType.MESH,
        )

    def take_own(side):
        return pltpu.make_async_copy(
            x_ref.at[:, :, :, pl.ds(side * LANES, LANES)], lanes.at[side], own_in.at[side]
        )

    def keep_half():
        return pltpu.make_async_copy(lanes.at[0, run(me)], got.at[0, me], own_half)

    def keep_part(q):
        return pltpu.make_async_copy(
            lanes.at[1, me * chunks + q], got.at[1, me, q], own_part.at[q]
        )

    def give_own(q):
        return pltpu.make_async_copy(ready.at[place, part(q)], out_ref.at[place, part(q)], own_out.at[q])

    def begin(q):
        keep_part(q).start()
        others(devices, lambda step: everywhere(q, step).start())

    def transform(side):
        time_kernel(
            lanes.at[side], turn_ref, cos_t_ref, sin_t_ref,
            factor_ref.at[:, :, pl.ds(side * LANES, LANES)], fir_ref, lanes.at[side],
            line_held, padded,
        )

    take_own(0).start()
    take_own(1).start()
    greet(devices, owners, me)
    take_own(0).wait()
    transform(0)
    keep_half().start()
    others(devices, lambda step: half(step).start())
    take_own(1).wait()
    transform(1)
    ahead = min(2, chunks)
    for q in range(ahead):
        begin(q)
    keep_half().wait()
    others(devices, lambda step: half(step, True).wait_recv())

    @pl.loop(0, chunks)
    def _(q):
        keep_part(q).wait()
        others(devices, lambda step: everywhere(q, step, True).wait_recv())

        @pl.when(q + ahead < chunks)
        def _():
            begin(q + ahead)

        def load(at):
            return jnp.concatenate([got[side, at, q, p] for p in range(2) for side in range(2)], axis=-1)

        inverse_body(
            load, table_ref, first_ref, cos_ref, sin_ref,
            ready.at[:, part(q)], held,
        )
        give_own(q).start()
        for step in range(1, owners):
            across(q, step).start()

    others(devices, lambda step: half(step).wait_send())

    @pl.loop(0, chunks)
    def _(q):
        others(devices, lambda step: everywhere(q, step).wait_send())
        give_own(q).wait()
        for step in range(1, owners):
            across(q, step).wait_send()
            across(q, step, True).wait_recv()


CHUNK = 16


def exchange_semaphores(chunks, owners, devices):
    dma = pltpu.SemaphoreType.DMA
    return [
        dma((chunks,)), dma((chunks,)), dma((chunks, owners)), dma((chunks, owners)),
        dma((chunks, devices)), dma((chunks, devices)),
    ]


def exchange_call(kernel, ident, operands, out_shape, scratch):
    anywhere = pl.BlockSpec(memory_space=pl.ANY)
    inside = pl.BlockSpec(memory_space=pltpu.VMEM)
    return pl.pallas_call(
        kernel,
        in_specs=[anywhere] + [inside] * (len(operands) - 1),
        out_specs=anywhere,
        out_shape=jax.ShapeDtypeStruct(out_shape, F32),
        scratch_shapes=scratch,
        compiler_params=pltpu.CompilerParams(
            vmem_limit_bytes=56 * 2**20, collective_id=ident, has_side_effects=True
        ),
        name=kernel.__name__,
    )(*operands)


def send_out(x, devices):
    owners, rows, width = x.shape
    channels = owners * width
    slots = channels // WIDE // 2
    block = min(CHUNK, rows)
    chunks = rows // block
    table, first, cos, sin = channel_tables(channels)
    operands = [x] + [jnp.asarray(t) for t in (halves(table), halves(first), cos, sin)]
    buffers = [(owners, rows, width), (slots, block, 2 * WIDE), (chunks, slots, 2, block, WIDE)]
    scratch = [pltpu.VMEM(b, F32) for b in buffers] + exchange_semaphores(chunks, owners, devices)
    return exchange_call(send_out_kernel, 0, operands, (devices * chunks, 2, block, WIDE), scratch)


def send_back(x, factor, taps, owners, devices, channels):
    pieces, _, block, _ = x.shape
    samples = pieces * block
    slots = channels // WIDE // 2
    chunks = pieces // devices
    rows = chunks * block
    table, first, cos, sin = channel_tables(channels)
    operands = [x, *time_tables(samples), factor, fir_table(taps)]
    operands += [jnp.asarray(t) for t in (halves(table.T), halves(first.T), cos, sin)]
    shape = (owners, rows, channels // owners)
    buffers = [
        (2, pieces, 2, block, LANES), (2, samples // WIDE, WIDE, LANES),
        (2, samples + 2 * LANES, LANES), (2, devices, chunks, 2, block, LANES),
        (slots, block, 2 * WIDE), shape,
    ]
    dma = pltpu.SemaphoreType.DMA
    scratch = [pltpu.VMEM(b, F32) for b in buffers]
    scratch += [dma((2,)), dma(()), dma((chunks,)), dma((chunks,)), dma((devices,)), dma((devices,))]
    scratch += exchange_semaphores(chunks, owners, devices)[2:]
    return exchange_call(send_back_kernel, 1, operands, shape, scratch)


def time_kernel(x_ref, table_ref, cos_ref, sin_ref, factor_ref, fir_ref, out_ref, held, line):
    devices, _, rows, lanes = x_ref.shape
    radix = held.shape[1]
    per = WIDE // rows

    @pl.loop(0, WIDE // 8)
    def _(tile):
        part = tile // (rows // 8)
        at = pl.ds(pl.multiple_of(lax.rem(tile, rows // 8) * 8, 8), 8)
        to = pl.ds(pl.multiple_of(tile * 8, 8), 8)
        x = [(x_ref[b * per + part, 0, at], x_ref[b * per + part, 1, at]) for b in range(radix)]
        y = complex_short(x, -1.0)
        for g in range(radix):
            re, im = y[g]
            c, s = cos_ref[g, to], sin_ref[g, to]
            held[0, g, to] = re * c + im * s
            held[1, g, to] = im * c - re * s

    group = min(4, radix)

    def columns(y, k):
        return y[:, k * lanes : (k + 1) * lanes]

    @pl.loop(0, radix // group)
    def _(step):
        gs = [step * group + k for k in range(group)]
        x = jnp.concatenate([held[p, g] for g in gs for p in range(2)], axis=1)
        y = dot_left(table_ref, x)
        parts = []
        for k, g in enumerate(gs):
            factor = factor_ref[g]
            cr, ci = columns(y[:WIDE], 2 * k), columns(y[:WIDE], 2 * k + 1)
            sr, si = columns(y[WIDE:], 2 * k), columns(y[WIDE:], 2 * k + 1)
            parts += [(cr + si) * factor, (ci - sr) * factor]
        y = dot_left(table_ref, jnp.concatenate(parts, axis=1))
        for k, g in enumerate(gs):
            cr, ci = columns(y[:WIDE], 2 * k), columns(y[:WIDE], 2 * k + 1)
            sr, si = columns(y[WIDE:], 2 * k), columns(y[WIDE:], 2 * k + 1)
            re, im = cr - si, ci + sr
            c, s = cos_ref[g], sin_ref[g]
            held[0, g] = re * c - im * s
            held[1, g] = im * c + re * s

    edge = line.shape[1] - LANES
    for part in range(2):
        line[part, :LANES] = jnp.zeros((LANES, lanes), F32)
        line[part, edge:] = jnp.zeros((LANES, lanes), F32)

    @pl.loop(0, WIDE // 8)
    def _(tile):
        at = pl.ds(pl.multiple_of(tile * 8, 8), 8)
        y = complex_short([(held[0, g, at], held[1, g, at]) for g in range(radix)], 1.0)
        for b in range(radix):
            to = pl.ds(pl.multiple_of(LANES + b * WIDE + tile * 8, 8), 8)
            line[0, to] = y[b][0]
            line[1, to] = y[b][1]

    @pl.loop(0, radix // group)
    def _(step):
        bs = [step * group + k for k in range(group)]
        x = [
            line[p, pl.ds(pl.multiple_of(b * WIDE, WIDE), 2 * WIDE)] for b in bs for p in range(2)
        ]
        y = dot_left(fir_ref, jnp.concatenate(x, axis=1))
        for k, b in enumerate(bs):
            to = pl.ds(b * per, per)
            out_ref[to, 0] = columns(y, 2 * k).reshape(per, rows, lanes)
            out_ref[to, 1] = columns(y, 2 * k + 1).reshape(per, rows, lanes)


def fir_table(taps):
    count = taps.shape[0]
    shift = LANES - (count - 1) // 2
    period = 2 * WIDE + 1
    row = jnp.pad(taps, (shift, period - count - shift))
    table = jnp.tile(row, WIDE)[: WIDE * 2 * WIDE].reshape(WIDE, 2 * WIDE)
    high = lax.reduce_precision(table, 8, 7)
    return jnp.stack([high, table - high]).astype(jnp.bfloat16)


def time_tables(samples):
    radix = samples // WIDE
    a = np.arange(WIDE)
    cos, sin = turn(a[:, None] * a[None, :], WIDE)
    table = jnp.asarray(halves(np.concatenate([cos, sin], axis=0)))
    spread = (radix, WIDE, LANES)
    turns = turn(np.arange(radix)[:, None] * a[None, :], samples)
    return [table] + [
        jnp.asarray(np.broadcast_to(t.astype(np.float32)[:, :, None], spread)) for t in turns
    ]


def time_stage(x, factor, taps):
    devices, _, rows, piece = x.shape
    samples = devices * rows
    radix = samples // WIDE
    table, *turns = time_tables(samples)
    fir = fir_table(taps)
    block = pl.BlockSpec((devices, 2, rows, LANES), lambda i: (0, 0, 0, i))
    return pl.pallas_call(
        time_kernel,
        grid=(piece // LANES,),
        in_specs=[
            block,
            whole(table.shape),
            whole(turns[0].shape),
            whole(turns[1].shape),
            pl.BlockSpec((radix, WIDE, LANES), lambda i: (0, 0, i)),
            whole(fir.shape),
        ],
        out_specs=block,
        out_shape=jax.ShapeDtypeStruct(x.shape, F32),
        scratch_shapes=[
            pltpu.VMEM((2, radix, WIDE, LANES), F32),
            pltpu.VMEM((2, samples + 2 * LANES, LANES), F32),
        ],
        compiler_params=params(),
        name="time_stage",
    )(x, table, *turns, factor, fir)


def mask_factor(band_edges, channels, piece, width):
    samples = band_edges.shape[1]
    owner = lax.axis_index("tm") * lax.axis_size("chan") + lax.axis_index("chan")
    order = jnp.asarray(wave_order(channels))
    wave = lax.dynamic_slice_in_dim(order, owner * piece, piece)
    wave = jnp.pad(wave, (0, width - piece))[None, None, :]
    edges = band_edges.reshape(2, WIDE, samples // WIDE).transpose(0, 2, 1)[:, :, :, None]
    kept = (wave >= edges[0]) & (wave <= edges[1])
    weight = jnp.where(wave == 0, 1.0, 2.0).astype(F32)
    return jnp.where(kept, weight, 0.0) / float(samples * channels)


def regroup(x, devices):
    slots, _, rows, _ = x.shape
    share = devices // slots
    if share == 1:
        return x
    x = x.reshape(slots, 2, rows, share, WIDE // share).transpose(0, 3, 1, 2, 4)
    return x.reshape(devices, 2, rows, WIDE // share)


def ungroup(x, slots):
    devices, _, rows, piece = x.shape
    share = devices // slots
    if share == 1:
        return x
    x = x.reshape(slots, share, 2, rows, piece).transpose(0, 2, 3, 1, 4)
    return x.reshape(slots, 2, rows, WIDE)


def exchange(x, axes):
    return lax.all_to_all(x, axes, split_axis=0, concat_axis=0, tiled=True)


def per_device(traces, band_edges, taps, gain_table, gain_index):
    owners = lax.axis_size("chan")
    devices = lax.axis_size("tm") * owners
    length, width = traces.shape
    channels = owners * width
    slots = channels // WIDE // 2
    piece = channels // 2 // devices
    padded = max(piece, LANES)
    matches = gain_index[:, None] == jnp.arange(gain_table.shape[0], dtype=jnp.int32)[None, :]
    gains = jnp.sum(jnp.where(matches, gain_table[None, :], 0.0), axis=1)
    factor = mask_factor(band_edges, channels, piece, padded)

    if devices == slots:
        spectra = send_out(traces.reshape(owners, length // owners, width), devices)
        local = send_back(spectra, factor, taps, owners, devices, channels)
        return local.reshape(length, width) * gains[None, :]

    gathered = exchange(traces.reshape(owners, length // owners, width), "chan")
    spectra = exchange(regroup(channel_forward(gathered), devices), AXES)
    if padded > piece:
        spectra = jnp.pad(spectra, ((0, 0), (0, 0), (0, 0), (0, padded - piece)))
    spectra = time_stage(spectra, factor, taps)
    if padded > piece:
        spectra = spectra[..., :piece]
    returned = ungroup(exchange(spectra, AXES), slots)
    local = exchange(channel_inverse(returned, owners), "chan")
    return local.reshape(length, width) * gains[None, :]


def solution(mesh):
    in_specs = (P("tm", "chan"), P(), P(), P(), P("chan"))
    out_specs = P("tm", "chan")
    return jax.shard_map(
        per_device, mesh=mesh, in_specs=in_specs, out_specs=out_specs, check_vma=False
    )
```
